512 devices in a mesh: row: 16 (over y, core), col: 32 (over x, z).
Axes of the slice: x: 4, y: 8, z: 8, core: 2. Of those that a mesh axis runs over, the one named last changes fastest.
Arguments:
- momentum: bfloat16 [8192, 36864], P('row', 'col'), may hold values from -6 to 6
- gradient: bfloat16 [8192, 36864], P('row', 'col'), may hold values from -250 to 250
- right_factor: float32 [36864, 256], P(('col', 'row')), may hold values from -0.03125 to 0.03125
Outputs:
- new_momentum: bfloat16 [8192, 36864], P('row', 'col')
- step_update: bfloat16 [8192, 36864], P('row', 'col')
- new_right_factor: float32 [36864, 256], P(('col', 'row'))
The draws below stay inside these ranges and needn't reach their ends.
All inputs are finite; a program needn't handle non-finite values.
Results may differ from the reference program's by a relative error of at most 0.012.
Values may be sent and summed in bfloat16 or wider, within the bound.
A program may use at most 64 MiB of HBM per device.

```python
import math
import jax
import jax.numpy as jnp
from jax import lax

RANK = 256
ROWS = 8192
COLS = 36864


def draw_gradient(key, part):
    key = jax.random.fold_in(key, 11)
    keys = jax.random.split(key, 3)
    row_ramp = (1.0 + 2.0 * jnp.arange(ROWS, dtype=jnp.float32) / (ROWS - 1)) / math.sqrt(3.0)
    col_ramp = (1.0 + 2.0 * jnp.arange(COLS, dtype=jnp.float32) / (COLS - 1)) / math.sqrt(3.0)
    row_scale = jnp.exp(jax.random.uniform(keys[0], (ROWS,), jnp.float32, 0.0, math.log(10.0))) / math.sqrt(10.0) * row_ramp
    col_scale = jnp.exp(jax.random.uniform(keys[1], (COLS,), jnp.float32, 0.0, math.log(10.0))) / math.sqrt(10.0) * col_ramp
    values = jax.random.truncated_normal(keys[2], -6.0, 6.0, (ROWS, COLS), jnp.float32)
    return (values * row_scale[:, None] * col_scale[None, :]).astype(jnp.bfloat16)


def block_levels(stream_key, extent, cuts, low, largest):
    def one(position, shards_of):
        draws = jax.random.uniform(jax.random.fold_in(jax.random.fold_in(stream_key, 6), position), (shards_of,), jnp.float32, low / len(cuts), largest / len(cuts))
        return jnp.repeat(jnp.exp(draws), extent[position] // shards_of).reshape((-1,) + (1,) * (len(extent) - position - 1))

    level = one(*cuts[0])
    for cut in cuts[1:]:
        level = level * one(*cut)
    return level


def centred(stream_key, extent, deviation, limit, cuts=(), kind=jnp.bfloat16):
    result = deviation * jax.random.normal(stream_key, extent, jnp.float32)
    if cuts:
        result = result * block_levels(stream_key, extent, cuts, -0.22, 0.18)
    return jnp.clip(result, -limit, limit).astype(kind)


def setup_inputs(seed: int = 0) -> dict:
    streams_of = jax.random.split(jax.random.key(seed), 4)
    momentum = centred(streams_of[0], (ROWS, COLS), 1.0, 6.0, ((0, 16), (1, 32)))
    gradient = draw_gradient(jax.random.fold_in(streams_of[3], 71), 0)
    right_factor = centred(streams_of[2], (COLS, RANK), COLS ** -0.5, 0.03125, ((0, 512),), jnp.float32)
    return {"momentum": momentum, "gradient": gradient, "right_factor": right_factor}


def reference(momentum, gradient, right_factor):
    buffer = (momentum.astype(jnp.float32) + gradient.astype(jnp.float32)).astype(jnp.bfloat16)
    factor_low = right_factor.astype(jnp.bfloat16)
    left_panel = jnp.dot(buffer.astype(jnp.float32), factor_low.astype(jnp.float32), preferred_element_type=jnp.float32)
    gram_matrix = lax.dot_general(left_panel, left_panel, (((0,), (0,)), ((), ())), precision=lax.Precision.HIGHEST)
    lower = jnp.linalg.cholesky(gram_matrix)
    left_basis = lax.linalg.triangular_solve(lower, left_panel, left_side=False, lower=True, transpose_a=True).astype(jnp.bfloat16)
    coefficients = lax.dot_general(buffer.astype(jnp.float32), left_basis.astype(jnp.float32), (((0,), (0,)), ((), ())), preferred_element_type=jnp.float32)
    column_norms = lax.optimization_barrier(jnp.sum(coefficients * coefficients, axis=0))
    inverse = 1.0 / jnp.sqrt(column_norms + 1e-06)
    new_right_factor = coefficients * inverse
    coeff_low = coefficients.astype(jnp.bfloat16)
    factor_next = new_right_factor.astype(jnp.bfloat16)
    correction = lax.dot_general(left_basis.astype(jnp.float32), coeff_low.astype(jnp.float32), (((1,), (1,)), ((), ())), preferred_element_type=jnp.float32)
    new_momentum = (buffer.astype(jnp.float32) - 0.05 * correction).astype(jnp.bfloat16)
    update_scale = math.sqrt(ROWS * COLS / RANK)
    direction = lax.dot_general(left_basis.astype(jnp.float32), factor_next.astype(jnp.float32), (((1,), (1,)), ((), ())), preferred_element_type=jnp.float32)
    step_update = (update_scale * direction).astype(jnp.bfloat16)
    return (new_momentum, step_update, new_right_factor)
```

```python
import functools
import math

import jax
import jax.numpy as jnp
from jax import lax
from jax.experimental import pallas as pl
from jax.experimental.pallas import tpu as pltpu
from jax.sharding import PartitionSpec as P

MESH = pl.DeviceIdType.MESH
LANES = 128
X_CHIPS = 4
F32 = jnp.float32
BF16 = jnp.bfloat16


def dot(a, b):
    return jnp.dot(a, b, preferred_element_type=F32)


def dot_nt(a, b):
    return lax.dot_general(a, b, (((1,), (1,)), ((), ())), preferred_element_type=F32)


def split(value):
    high = value.astype(BF16)
    return high, (value - high.astype(F32)).astype(BF16)


def splat(rows, lane):
    return jnp.broadcast_to(rows[:, lane : lane + 1], (rows.shape[0], LANES))


def eliminate(block):
    n = LANES
    lanes = lax.broadcasted_iota(jnp.int32, (8, LANES), 1)
    sublane = lax.broadcasted_iota(jnp.int32, (8, LANES), 0)
    groups = [block[8 * g : 8 * g + 8, :] for g in range(n // 8)]
    for j in range(n // 8):
        base = 8 * j
        inside = (lanes >= base) & (lanes < base + 8)
        rows = [jnp.broadcast_to(groups[j][k : k + 1, :], (8, LANES)) for k in range(8)]
        entry = {(i, k): splat(rows[k], base + i) for k in range(8) for i in range(k, 8)}
        rows = [jnp.where(inside, jnp.where(lanes == base + k, 1.0, 0.0), rows[k]) for k in range(8)]
        low, inv = {}, {}
        for k in range(8):
            root = lax.rsqrt(entry[k, k])
            for i in range(k + 1, 8):
                low[i, k] = entry[i, k] * root
            for m in range(k + 1, 8):
                for i in range(m, 8):
                    entry[i, m] = entry[i, m] - low[i, k] * low[m, k]
            rows[k] = rows[k] * root
            for i in range(k + 1, 8):
                rows[i] = rows[i] - low[i, k] * rows[k]
            inv[k, k] = root
            for i in range(k):
                total = low[k, i] * inv[i, i]
                for m in range(i + 1, k):
                    total = total + low[k, m] * inv[m, i]
                inv[k, i] = -(total * root)
        value = rows[0]
        for k in range(1, 8):
            value = jnp.where(sublane == k, rows[k], value)
        groups[j] = value
        if j == n // 8 - 1:
            break
        back = []
        for i in range(8):
            terms = [inv[k, i] * rows[k] for k in range(i, 8)]
            while len(terms) > 1:
                terms = [sum(terms[a : a + 2][1:], terms[a]) for a in range(0, len(terms), 2)]
            back.append(terms[0])
        for g in range(j + 1, n // 8):
            columns = [splat(groups[g], base + k) for k in range(8)]
            terms = [columns[k] * back[k] for k in range(8)]
            while len(terms) > 1:
                terms = [terms[a] + terms[a + 1] for a in range(0, len(terms), 2)]
            groups[g] = jnp.where(inside, 0.0, groups[g]) - terms[0]
    whole = jnp.concatenate(groups, axis=0)
    at_row = lax.broadcasted_iota(jnp.int32, (n, n), 0)
    at_col = lax.broadcasted_iota(jnp.int32, (n, n), 1)
    return jnp.where(at_row >= at_col, whole, 0.0)


def exact(a, b, dims):
    return lax.dot_general(a, b, ((dims[:1], dims[1:]), ((), ())), precision=lax.Precision.HIGHEST)


def inverse_lower(work, out_ref, hook):
    top, rest = slice(0, LANES), slice(LANES, 2 * LANES)
    first = eliminate(work[top, top])
    out_ref[top, top] = first
    out_ref[top, rest] = jnp.zeros((LANES, LANES), F32)
    upper = exact(first, work[top, rest], (1, 0))
    schur = work[rest, rest] - exact(upper, upper, (0, 0))
    hook()
    second = eliminate(schur)
    out_ref[rest, rest] = second
    out_ref[rest, top] = -exact(second, exact(upper, first, (0, 0)), (1, 0))


def remote(src, dst, send, recv, device):
    return pltpu.make_async_remote_copy(
        src_ref=src, dst_ref=dst, send_sem=send, recv_sem=recv, device_id=device, device_id_type=MESH
    )


def step_kernel(
    sizes,
    momentum,
    gradient,
    factor,
    buf,
    basis_low,
    scaled_out,
    coeff_low,
    right_out,
    *scratch,
):
    ny, nx, nz, scale = sizes
    (
        grad, fown, fslot, fall, part, psend, xgot, zsend, zgot, panel, panel_t,
        gpart, ggot, gall, work, lower_inv, wpart, wsib, wsibgot, wsend, wgot, wall, coeff_t,
        nown, nxgot, nmid, nzgot,
        local_sem, f_send, f_recv, fs_send, fs_recv,
        x_send, x_recv, z_send, z_recv, pz_send, pz_recv, px_send, px_recv,
        gy_send, gy_recv, gz_send, gz_recv, gx_send, gx_recv, gs_send, gs_recv,
        ws_send, ws_recv, wy_send, wy_recv, wa_send, wa_recv, wf_send, wf_recv,
        nx_send, nx_recv, nz_send, nz_recv,
    ) = scratch
    row, col = lax.axis_index("row"), lax.axis_index("col")
    y, core = row // 2, row % 2
    x, z = col // nz, col % nz
    frows, rank = factor.shape
    rows_dev, cols_dev = buf.shape
    ncol = nx * nz
    sibling = (y * 2 + 1 - core, col)

    def at_y(d, flip=0):
        core_to = core if flip == 0 else 1 - core
        return (lax.rem(y + d, ny) * 2 + core_to, col)

    def at_x(d):
        return (row, lax.rem(x + d, nx) * nz + z)

    def at_z(d):
        return (row, x * nz + lax.rem(z + d, nz))

    started = []

    def send(copy):
        copy.start()
        started.append(copy)

    loads = [
        pltpu.make_async_copy(momentum, buf, local_sem.at[0]),
        pltpu.make_async_copy(gradient, grad, local_sem.at[1]),
        pltpu.make_async_copy(factor, fown, local_sem.at[2]),
    ]
    for copy in loads[::-1]:
        copy.start()

    peers = [at_y(d, flip) for d in range(ny) for flip in range(2) if (d, flip) != (0, 0)]
    peers += [at_x(d) for d in range(1, nx)] + [at_z(d) for d in range(1, nz)]
    barrier = pltpu.get_barrier_semaphore()
    for peer in peers:
        pl.semaphore_signal(barrier, inc=1, device_id=peer, device_id_type=MESH)
    loads[2].wait()
    fslot[row] = jnp.concatenate([fown[:, :LANES], fown[:, LANES:]], axis=0).astype(BF16)
    pl.semaphore_wait(barrier, len(peers))

    for d in sorted(range(1, ny), key=lambda d: -min(d, ny - d)):
        send(remote(fslot.at[row], fslot.at[row], f_send.at[d], f_recv.at[d], at_y(d)))
    send(remote(fslot.at[row], fslot.at[row], fs_send.at[0], fs_recv.at[0], sibling))
    loads[0].wait()
    loads[1].wait()

    def add_rows(i, carry):
        here = pl.ds(pl.multiple_of(i * 32, 32), 32)
        buf[here, :] = (buf[here, :].astype(F32) + grad[here, :].astype(F32)).astype(BF16)
        return carry

    lax.fori_loop(0, rows_dev // 32, add_rows, 0)

    def unpack(source):
        whole = fslot[source].astype(F32)
        here = pl.ds(pl.multiple_of(source * frows, 8), frows)
        fall[here, :LANES] = whole[:frows]
        fall[here, LANES:] = whole[frows:]

    unpack(row)
    near = sorted(range(1, ny), key=lambda d: min(d, ny - d))
    for d in near:
        source = lax.rem(y + ny - d, ny) * 2 + core
        remote(fslot.at[source], fslot.at[source], f_send.at[d], f_recv.at[d], at_y(ny - d)).wait_recv()
        send(remote(fslot.at[source], fslot.at[source], fs_send.at[d], fs_recv.at[d], sibling))
        unpack(source)
    for d in [0] + near:
        source = lax.rem(y + ny - d, ny) * 2 + 1 - core
        remote(fslot.at[source], fslot.at[source], fs_send.at[d], fs_recv.at[d], sibling).wait_recv()
        unpack(source)

    prow = rows_dev // ncol
    right = fall[...].astype(BF16)
    many = rows_dev // nx
    halves_z = [pl.ds(h * (nz // 2), nz // 2) for h in range(2)]
    for dx in list(range(1, nx)) + [0]:
        group = lax.rem(x + dx, nx)
        value = dot(buf[pl.ds(pl.multiple_of(group * many, many), many), :], right)
        if dx == 0:
            part[...] = value.reshape(nz, prow, rank)
            continue
        psend[dx] = value.astype(BF16).reshape(nz, prow, rank)
        for h in range(2):
            src, dst = psend.at[dx, halves_z[h]], xgot.at[dx, halves_z[h]]
            send(remote(src, dst, x_send.at[dx, h], x_recv.at[dx, h], at_x(dx)))
    for h in range(2):
        here = halves_z[h]
        value = part[here]
        for dx in range(1, nx):
            got = xgot.at[dx, here]
            remote(got, got, x_send.at[dx, h], x_recv.at[dx, h], at_x(dx)).wait_recv()
            value = value + xgot[dx, here].astype(F32)
        part[here] = value
        zsend[here] = value.astype(BF16)
        for i in range(nz // 2):
            to = h * (nz // 2) + i
            away = lax.rem(to - z + nz, nz)

            @pl.when(away != 0)
            def _(to=to, away=away):
                copy = remote(zsend.at[to], zgot.at[away], z_send.at[away], z_recv.at[away], (row, x * nz + to))
                copy.start()

    value = part[z]
    for dz in range(1, nz):
        remote(zgot.at[dz], zgot.at[dz], z_send.at[dz], z_recv.at[dz], at_z(dz)).wait_recv()
        value = value + zgot[dz].astype(F32)
    panel[col] = value.astype(BF16)
    for dz in sorted(range(1, nz), key=lambda d: -min(d, nz - d)):
        send(remote(panel.at[col], panel.at[col], pz_send.at[dz], pz_recv.at[dz], at_z(dz)))
    for step in range(2):
        lot = z // (nz // 2) if step == 0 else 1 - z // (nz // 2)
        for i in range(nz // 2):
            source = lot * (nz // 2) + i
            away = lax.rem(z - source + nz, nz)
            got = panel.at[x * nz + source]

            @pl.when(away != 0)
            def _(got=got, away=away):
                remote(got, got, pz_send.at[away], pz_recv.at[away], at_z(1)).wait_recv()

        group = panel.at[pl.ds(x * nz + lot * (nz // 2), nz // 2)]
        for dx in range(1, nx):
            send(remote(group, group, px_send.at[dx, step], px_recv.at[dx, step], at_x(dx)))
    for step in range(2):
        lot = z // (nz // 2) if step == 0 else 1 - z // (nz // 2)
        for dx in range(1, nx):
            group = panel.at[pl.ds(lax.rem(x + nx - dx, nx) * nz + lot * (nz // 2), nz // 2)]
            remote(group, group, px_send.at[dx, step], px_recv.at[dx, step], at_x(dx)).wait_recv()
    for dz in range(1, nz):
        got = zsend.at[lax.rem(z + dz, nz)]
        remote(got, got, z_send.at[dz], z_recv.at[dz], at_z(dz)).wait_send()

    left = panel[...].reshape(rows_dev, rank)
    left_t = left.T
    halves = rank // 2
    panel_t[...] = left_t.reshape(2, halves, rows_dev)
    grow = rank // ncol
    gram = dot(left_t, left)
    for h in range(2):
        gpart[h] = gram[:, h * LANES : (h + 1) * LANES].reshape(ncol, grow, LANES)
    gpeers = [(d, flip) for d in range(ny) for flip in range(2) if (d, flip) != (0, 0)]
    for d, flip in gpeers:
        half = core if flip == 0 else 1 - core
        send(remote(gpart.at[half, col], ggot.at[d, flip], gy_send.at[d, flip], gy_recv.at[d, flip], at_y(d, flip)))

    wrow = halves // ny
    value = dot(panel_t[1 - core], buf[...])
    wsib[...] = value.astype(BF16).reshape(ny, wrow, cols_dev)
    for d in list(range(1, ny)) + [0]:
        piece = lax.rem(y + d, ny)
        send(remote(wsib.at[piece], wsibgot.at[d], ws_send.at[d], ws_recv.at[d], sibling))
    value = dot(panel_t[core], buf[...])
    wpart[...] = value.reshape(ny, wrow, cols_dev)

    value = gpart[core, col]
    for d, flip in gpeers:
        remote(ggot.at[d, flip], ggot.at[d, flip], gy_send.at[d, flip], gy_recv.at[d, flip], at_y(d, flip)).wait_recv()
        value = value + ggot[d, flip]
    gall[core, col] = value
    for dz in range(1, nz):
        send(remote(gall.at[core, col], gall.at[core, col], gz_send.at[dz], gz_recv.at[dz], at_z(dz)))

    def merged(d):
        remote(wsibgot.at[d], wsibgot.at[d], ws_send.at[d], ws_recv.at[d], sibling).wait_recv()
        return wpart[lax.rem(y + d, ny)] + wsibgot[d].astype(F32)

    for d in sorted(range(1, ny), key=lambda d: -min(d, ny - d)):
        wsend[d] = merged(d).astype(BF16)
        send(remote(wsend.at[d], wgot.at[d], wy_send.at[d], wy_recv.at[d], at_y(d)))

    for dz in range(1, nz):
        got = gall.at[core, x * nz + lax.rem(z + nz - dz, nz)]
        remote(got, got, gz_send.at[dz], gz_recv.at[dz], at_z(dz)).wait_recv()
    group = gall.at[core, pl.ds(x * nz, nz)]
    for dx in range(1, nx):
        send(remote(group, group, gx_send.at[dx], gx_recv.at[dx], at_x(dx)))
    for dx in range(1, nx):
        group = gall.at[core, pl.ds(lax.rem(x + nx - dx, nx) * nz, nz)]
        remote(group, group, gx_send.at[dx], gx_recv.at[dx], at_x(dx)).wait_recv()
    send(remote(gall.at[core], gall.at[core], gs_send.at[0], gs_recv.at[0], sibling))
    remote(gall.at[1 - core], gall.at[1 - core], gs_send.at[0], gs_recv.at[0], sibling).wait_recv()
    for h in range(2):
        work[:, h * LANES : (h + 1) * LANES] = gall[h].reshape(rank, LANES)
    def finish_sum():
        value = merged(0)
        for d in range(1, ny):
            remote(wgot.at[d], wgot.at[d], wy_send.at[d], wy_recv.at[d], at_y(d)).wait_recv()
            value = value + wgot[d].astype(F32)
        mine = core * ny + y
        wall[mine] = value.astype(BF16)
        for d in sorted(range(1, ny), key=lambda d: -min(d, ny - d)):
            send(remote(wall.at[mine], wall.at[mine], wa_send.at[d], wa_recv.at[d], at_y(d)))
        send(remote(wall.at[mine], wall.at[mine], wf_send.at[0], wf_recv.at[0], sibling))

    def forward():
        for d in near:
            piece = core * ny + lax.rem(y + ny - d, ny)
            remote(wall.at[piece], wall.at[piece], wa_send.at[d], wa_recv.at[d], at_y(d)).wait_recv()
            send(remote(wall.at[piece], wall.at[piece], wf_send.at[d], wf_recv.at[d], sibling))

    inverse_lower(work, lower_inv, finish_sum)
    forward()
    high, low = split(lower_inv[...])
    basis = dot_nt(left, high) + dot_nt(left, low)
    basis_low[...] = basis.astype(BF16)
    for d in range(ny):
        piece = (1 - core) * ny + lax.rem(y + ny - d, ny)
        remote(wall.at[piece], wall.at[piece], wf_send.at[d], wf_recv.at[d], sibling).wait_recv()

    together = wall[...].reshape(rank, cols_dev)
    coeff_t[...] = dot(high, together) + dot(low, together)
    squares = jnp.zeros((rank, LANES), F32)
    for i in range(cols_dev // LANES):
        value = coeff_t[:, i * LANES : (i + 1) * LANES]
        squares = squares + value * value
    sums = squares.T
    value = sums[0:8]
    for i in range(1, LANES // 8):
        value = value + sums[8 * i : 8 * i + 8]
    nown[...] = value
    for dx in range(1, nx):
        send(remote(nown, nxgot.at[dx], nx_send.at[dx], nx_recv.at[dx], at_x(dx)))
    coeff_low[...] = coeff_t[...].astype(BF16)
    for dx in range(1, nx):
        remote(nxgot.at[dx], nxgot.at[dx], nx_send.at[dx], nx_recv.at[dx], at_x(dx)).wait_recv()
        value = value + nxgot[dx]
    nmid[...] = value
    for dz in range(1, nz):
        send(remote(nmid, nzgot.at[dz], nz_send.at[dz], nz_recv.at[dz], at_z(dz)))
    pick = lax.broadcasted_iota(jnp.int32, (frows, cols_dev), 1)
    pick = pick == lax.broadcasted_iota(jnp.int32, (frows, cols_dev), 0) + row * frows
    pick = jnp.where(pick, 1.0, 0.0).astype(BF16)
    c_high, c_low = split(coeff_t[...])
    mine = dot_nt(pick, c_high) + dot_nt(pick, c_low)
    for copy in started:
        copy.wait_send()
    for dz in range(1, nz):
        remote(nzgot.at[dz], nzgot.at[dz], nz_send.at[dz], nz_recv.at[dz], at_z(dz)).wait_recv()
        value = value + nzgot[dz]
    norms = jnp.sum(value, axis=0, keepdims=True)
    inverse = 1.0 / jnp.sqrt(norms + 1e-06)
    right_out[...] = mine * inverse
    scaled_out[...] = (basis * (inverse * scale)).astype(BF16)


def outputs_kernel(
    buffer, basis, scaled, coeff, right, momentum_out, update_out, right_out, momentum_low, update_low, sems, right_sem
):
    rows = momentum_low.shape[1]
    copies = [pltpu.make_async_copy(right, right_out, right_sem)]
    copies[0].start()
    for i in range(buffer.shape[0] // rows):
        here = slice(i * rows, (i + 1) * rows)
        update_low[i] = dot(scaled[here, :], coeff[...]).astype(BF16)
        copies.append(pltpu.make_async_copy(update_low.at[i], update_out.at[here], sems.at[0, i]))
        copies[-1].start()
        correction = dot(basis[here, :], coeff[...])
        momentum_low[i] = (buffer[here, :].astype(F32) - 0.05 * correction).astype(BF16)
        copies.append(pltpu.make_async_copy(momentum_low.at[i], momentum_out.at[here], sems.at[1, i]))
        copies[-1].start()
    for copy in copies:
        copy.wait()


def body(nx, momentum, gradient, right_factor):
    ny = lax.axis_size("row") // 2
    nz = lax.axis_size("col") // nx
    ncol = nx * nz
    rows_dev, cols_dev = momentum.shape
    frows, rank = right_factor.shape
    scale = math.sqrt(rows_dev * 2 * ny * cols_dev * ncol / rank)
    prow, grow, wrow = rows_dev // ncol, rank // ncol, rank // (2 * ny)
    sem = lambda *shape: pltpu.SemaphoreType.DMA(shape)
    scratch = [
        pltpu.VMEM((rows_dev, cols_dev), BF16),
        pltpu.VMEM((frows, rank), F32),
        pltpu.VMEM((2 * ny, 2 * frows, LANES), BF16),
        pltpu.VMEM((cols_dev, rank), F32),
        pltpu.VMEM((nz, prow, rank), F32),
        pltpu.VMEM((nx, nz, prow, rank), BF16),
        pltpu.VMEM((nx, nz, prow, rank), BF16),
        pltpu.VMEM((nz, prow, rank), BF16),
        pltpu.VMEM((nz, prow, rank), BF16),
        pltpu.VMEM((ncol, prow, rank), BF16),
        pltpu.VMEM((2, rank // 2, rows_dev), BF16),
        pltpu.VMEM((2, ncol, grow, LANES), F32),
        pltpu.VMEM((ny, 2, grow, LANES), F32),
        pltpu.VMEM((2, ncol, grow, LANES), F32),
        pltpu.VMEM((rank, rank), F32),
        pltpu.VMEM((rank, rank), F32),
        pltpu.VMEM((ny, wrow, cols_dev), F32),
        pltpu.VMEM((ny, wrow, cols_dev), BF16),
        pltpu.VMEM((ny, wrow, cols_dev), BF16),
        pltpu.VMEM((ny, wrow, cols_dev), BF16),
        pltpu.VMEM((ny, wrow, cols_dev), BF16),
        pltpu.VMEM((2 * ny, wrow, cols_dev), BF16),
        pltpu.VMEM((rank, cols_dev), F32),
        pltpu.VMEM((8, rank), F32),
        pltpu.VMEM((nx, 8, rank), F32),
        pltpu.VMEM((8, rank), F32),
        pltpu.VMEM((nz, 8, rank), F32),
        sem(3),
        sem(ny), sem(ny), sem(ny), sem(ny),
        sem(nx, 2), sem(nx, 2), sem(nz), sem(nz), sem(nz), sem(nz), sem(nx, 2), sem(nx, 2),
        sem(ny, 2), sem(ny, 2), sem(nz), sem(nz), sem(nx), sem(nx), sem(1), sem(1),
        sem(ny), sem(ny), sem(ny), sem(ny), sem(ny), sem(ny), sem(ny), sem(ny),
        sem(nx), sem(nx), sem(nz), sem(nz),
    ]
    momentum, gradient, right_factor = [
        pltpu.with_memory_space_constraint(value, pltpu.HBM) for value in (momentum, gradient, right_factor)
    ]
    whole = pl.BlockSpec(memory_space=pltpu.VMEM)
    hbm = pl.BlockSpec(memory_space=pltpu.HBM)
    buffer, basis, scaled, coeff, new_right = pl.pallas_call(
        functools.partial(step_kernel, (ny, nx, nz, scale)),
        out_shape=[
            jax.ShapeDtypeStruct((rows_dev, cols_dev), BF16),
            jax.ShapeDtypeStruct((rows_dev, rank), BF16),
            jax.ShapeDtypeStruct((rows_dev, rank), BF16),
            jax.ShapeDtypeStruct((rank, cols_dev), BF16),
            jax.ShapeDtypeStruct((frows, rank), F32),
        ],
        in_specs=[hbm] * 3,
        out_specs=[whole] * 5,
        scratch_shapes=scratch,
        compiler_params=pltpu.CompilerParams(
            collective_id=0, has_side_effects=True, vmem_limit_bytes=48 * 1024 * 1024
        ),
        name="panel_and_factor",
    )(momentum, gradient, right_factor)
    step = min(128, rows_dev)
    return pl.pallas_call(
        outputs_kernel,
        out_shape=[jax.ShapeDtypeStruct((rows_dev, cols_dev), BF16)] * 2
        + [jax.ShapeDtypeStruct((frows, rank), F32)],
        in_specs=[whole] * 5,
        out_specs=[hbm] * 3,
        scratch_shapes=[pltpu.VMEM((rows_dev // step, step, cols_dev), BF16)] * 2
        + [sem(2, rows_dev // step), pltpu.SemaphoreType.DMA],
        compiler_params=pltpu.CompilerParams(vmem_limit_bytes=32 * 1024 * 1024),
        name="momentum_and_update",
    )(buffer, basis, scaled, coeff, new_right)


def solution(mesh, nx=X_CHIPS):
    placed = (P("row", "col"), P("row", "col"), P(("col", "row"), None))
    return jax.shard_map(
        functools.partial(body, nx), mesh=mesh, in_specs=placed, out_specs=placed, check_vma=False
    )
```

```python
import functools
import math

import jax
import jax.numpy as jnp
from jax import lax
from jax.experimental import pallas as pl
from jax.experimental.pallas import tpu as pltpu
from jax.sharding import PartitionSpec as P

MESH = pl.DeviceIdType.MESH
LANES = 128
X_CHIPS = 4
F32 = jnp.float32
BF16 = jnp.bfloat16


def dot(a, b):
    return jnp.dot(a, b, preferred_element_type=F32)


def dot_nt(a, b):
    return lax.dot_general(a, b, (((1,), (1,)), ((), ())), preferred_element_type=F32)


def split(value):
    high = value.astype(BF16)
    return high, (value - high.astype(F32)).astype(BF16)


def splat(rows, lane):
    return jnp.broadcast_to(rows[:, lane : lane + 1], (rows.shape[0], LANES))


def eliminate(block):
    n = LANES
    lanes = lax.broadcasted_iota(jnp.int32, (8, LANES), 1)
    sublane = lax.broadcasted_iota(jnp.int32, (8, LANES), 0)
    groups = [block[8 * g : 8 * g + 8, :] for g in range(n // 8)]
    for j in range(n // 8):
        base = 8 * j
        inside = (lanes >= base) & (lanes < base + 8)
        rows = [jnp.broadcast_to(groups[j][k : k + 1, :], (8, LANES)) for k in range(8)]
        entry = {(i, k): splat(rows[k], base + i) for k in range(8) for i in range(k, 8)}
        rows = [jnp.where(inside, jnp.where(lanes == base + k, 1.0, 0.0), rows[k]) for k in range(8)]
        low, inv = {}, {}
        for k in range(8):
            root = lax.rsqrt(entry[k, k])
            for i in range(k + 1, 8):
                low[i, k] = entry[i, k] * root
            for m in range(k + 1, 8):
                for i in range(m, 8):
                    entry[i, m] = entry[i, m] - low[i, k] * low[m, k]
            rows[k] = rows[k] * root
            for i in range(k + 1, 8):
                rows[i] = rows[i] - low[i, k] * rows[k]
            inv[k, k] = root
            for i in range(k):
                total = low[k, i] * inv[i, i]
                for m in range(i + 1, k):
                    total = total + low[k, m] * inv[m, i]
                inv[k, i] = -(total * root)
        value = rows[0]
        for k in range(1, 8):
            value = jnp.where(sublane == k, rows[k], value)
        groups[j] = value
        if j == n // 8 - 1:
            break
        back = []
        for i in range(8):
            terms = [inv[k, i] * rows[k] for k in range(i, 8)]
            while len(terms) > 1:
                terms = [sum(terms[a : a + 2][1:], terms[a]) for a in range(0, len(terms), 2)]
            back.append(terms[0])
        for g in range(j + 1, n // 8):
            columns = [splat(groups[g], base + k) for k in range(8)]
            terms = [columns[k] * back[k] for k in range(8)]
            while len(terms) > 1:
                terms = [terms[a] + terms[a + 1] for a in range(0, len(terms), 2)]
            groups[g] = jnp.where(inside, 0.0, groups[g]) - terms[0]
    whole = jnp.concatenate(groups, axis=0)
    at_row = lax.broadcasted_iota(jnp.int32, (n, n), 0)
    at_col = lax.broadcasted_iota(jnp.int32, (n, n), 1)
    return jnp.where(at_row >= at_col, whole, 0.0)


def exact(a, b, dims):
    return lax.dot_general(a, b, ((dims[:1], dims[1:]), ((), ())), precision=lax.Precision.HIGHEST)


def inverse_lower(work, out_ref):
    top, rest = slice(0, LANES), slice(LANES, 2 * LANES)
    first = eliminate(work[top, top])
    out_ref[top, top] = first
    out_ref[top, rest] = jnp.zeros((LANES, LANES), F32)
    upper = exact(first, work[top, rest], (1, 0))
    schur = work[rest, rest] - exact(upper, upper, (0, 0))
    second = eliminate(schur)
    out_ref[rest, rest] = second
    out_ref[rest, top] = -exact(second, exact(upper, first, (0, 0)), (1, 0))


def remote(src, dst, send, recv, device):
    return pltpu.make_async_remote_copy(
        src_ref=src, dst_ref=dst, send_sem=send, recv_sem=recv, device_id=device, device_id_type=MESH
    )


def step_kernel(
    sizes,
    momentum,
    gradient,
    factor,
    buf,
    basis_low,
    scaled_out,
    coeff_low,
    right_out,
    *scratch,
):
    ny, nx, nz, scale = sizes
    (
        grad, fown, fslot, fall, part, psend, xgot, zsend, zgot, panel, panel_t,
        gpart, ggot, gall, work, lower_inv, wpart, wsib, wsibgot, wsend, wgot, wall, coeff_t,
        nown, ngot,
        local_sem, f_send, f_recv, fs_send, fs_recv,
        x_send, x_recv, z_send, z_recv, pz_send, pz_recv, px_send, px_recv,
        gy_send, gy_recv, gx_send, gx_recv, gs_send, gs_recv,
        ws_send, ws_recv, wy_send, wy_recv, wa_send, wa_recv, wf_send, wf_recv,
        n_send, n_recv,
    ) = scratch
    row, col = lax.axis_index("row"), lax.axis_index("col")
    y, core = row // 2, row % 2
    x, z = col // nz, col % nz
    frows, rank = factor.shape
    rows_dev, cols_dev = buf.shape
    ncol = nx * nz
    sibling = (y * 2 + 1 - core, col)

    def at_y(d, flip=0):
        core_to = core if flip == 0 else 1 - core
        return (lax.rem(y + d, ny) * 2 + core_to, col)

    def at_x(d):
        return (row, lax.rem(x + d, nx) * nz + z)

    def at_z(d):
        return (row, x * nz + lax.rem(z + d, nz))

    def col_of(dx, dz):
        return lax.rem(x + dx + nx, nx) * nz + lax.rem(z + dz + nz, nz)

    def at_xz(dx, dz):
        return (row, col_of(dx, dz))

    started = []

    def send(copy):
        copy.start()
        started.append(copy)

    loads = [
        pltpu.make_async_copy(momentum, buf, local_sem.at[0]),
        pltpu.make_async_copy(gradient, grad, local_sem.at[1]),
        pltpu.make_async_copy(factor, fown, local_sem.at[2]),
    ]
    for copy in loads[::-1]:
        copy.start()

    peers = [at_y(d, flip) for d in range(ny) for flip in range(2) if (d, flip) != (0, 0)]
    col_peers = [(dx, dz) for dx in range(nx) for dz in range(nz) if (dx, dz) != (0, 0)]
    col_peers.sort(key=lambda d: -min(d[0], nx - d[0]) - min(d[1], nz - d[1]))
    peers += [at_xz(*d) for d in col_peers]
    barrier = pltpu.get_barrier_semaphore()
    for peer in peers:
        pl.semaphore_signal(barrier, inc=1, device_id=peer, device_id_type=MESH)
    loads[2].wait()
    fslot[row] = jnp.concatenate([fown[:, :LANES], fown[:, LANES:]], axis=0).astype(BF16)
    pl.semaphore_wait(barrier, len(peers))

    for d in sorted(range(1, ny), key=lambda d: -min(d, ny - d)):
        send(remote(fslot.at[row], fslot.at[row], f_send.at[d], f_recv.at[d], at_y(d)))
    send(remote(fslot.at[row], fslot.at[row], fs_send.at[0], fs_recv.at[0], sibling))
    loads[0].wait()
    loads[1].wait()

    def add_rows(i, carry):
        here = pl.ds(pl.multiple_of(i * 32, 32), 32)
        buf[here, :] = (buf[here, :].astype(F32) + grad[here, :].astype(F32)).astype(BF16)
        return carry

    lax.fori_loop(0, rows_dev // 32, add_rows, 0)

    def unpack(source):
        whole = fslot[source].astype(F32)
        here = pl.ds(pl.multiple_of(source * frows, 8), frows)
        fall[here, :LANES] = whole[:frows]
        fall[here, LANES:] = whole[frows:]

    unpack(row)
    near = sorted(range(1, ny), key=lambda d: min(d, ny - d))
    for d in near:
        source = lax.rem(y + ny - d, ny) * 2 + core
        remote(fslot.at[source], fslot.at[source], f_send.at[d], f_recv.at[d], at_y(ny - d)).wait_recv()
        send(remote(fslot.at[source], fslot.at[source], fs_send.at[d], fs_recv.at[d], sibling))
        unpack(source)
    for d in [0] + near:
        source = lax.rem(y + ny - d, ny) * 2 + 1 - core
        remote(fslot.at[source], fslot.at[source], fs_send.at[d], fs_recv.at[d], sibling).wait_recv()
        unpack(source)

    prow = rows_dev // ncol
    right = fall[...].astype(BF16)
    many = rows_dev // nx
    order = sorted(range(1, nz), key=lambda d: -min(d, nz - d)) + [0]
    for dx in list(range(1, nx)) + [0]:
        group = lax.rem(x + dx, nx)
        value = dot(buf[pl.ds(pl.multiple_of(group * many, many), many), :], right).reshape(nz, prow, rank)
        if dx == 0:
            part[...] = value
            continue
        psend[dx] = value.astype(BF16)
        for dz in order:
            src = psend.at[dx, lax.rem(z + dz, nz)]
            send(remote(src, xgot.at[dx, dz], x_send.at[dx, dz], x_recv.at[dx, dz], at_x(dx)))
    for dz in order:
        value = part[lax.rem(z + dz, nz)]
        for dx in range(1, nx):
            remote(xgot.at[dx, dz], xgot.at[dx, dz], x_send.at[dx, dz], x_recv.at[dx, dz], at_x(dx)).wait_recv()
            value = value + xgot[dx, dz].astype(F32)
        if dz:
            zsend[dz] = value.astype(BF16)
            send(remote(zsend.at[dz], zgot.at[dz], z_send.at[dz], z_recv.at[dz], at_z(dz)))
    for dz in sorted(range(1, nz), key=lambda d: min(d, nz - d)):
        remote(zgot.at[dz], zgot.at[dz], z_send.at[dz], z_recv.at[dz], at_z(dz)).wait_recv()
        value = value + zgot[dz].astype(F32)
    panel[col] = value.astype(BF16)
    for dz in order[:-1]:
        send(remote(panel.at[col], panel.at[col], pz_send.at[dz], pz_recv.at[dz], at_z(dz)))
    for dz in [0] + sorted(range(1, nz), key=lambda d: min(d, nz - d)):
        piece = x * nz + lax.rem(z + nz - dz, nz)
        if dz:
            remote(panel.at[piece], panel.at[piece], pz_send.at[dz], pz_recv.at[dz], at_z(dz)).wait_recv()
        for dx in range(1, nx):
            send(remote(panel.at[piece], panel.at[piece], px_send.at[dx, dz], px_recv.at[dx, dz], at_x(dx)))
    for dz in range(nz):
        for dx in range(1, nx):
            piece = lax.rem(x + nx - dx, nx) * nz + lax.rem(z + nz - dz, nz)
            remote(panel.at[piece], panel.at[piece], px_send.at[dx, dz], px_recv.at[dx, dz], at_x(dx)).wait_recv()

    left = panel[...].reshape(rows_dev, rank)
    left_t = left.T
    halves = rank // 2
    panel_t[...] = left_t.reshape(2, halves, rows_dev)

    wrow = halves // ny
    value = dot(panel_t[1 - core], buf[...])
    wsib[...] = value.astype(BF16).reshape(ny, wrow, cols_dev)
    for d in sorted(range(ny), key=lambda d: -min(d, ny - d)):
        piece = lax.rem(y + d, ny)
        send(remote(wsib.at[piece], wsibgot.at[d], ws_send.at[d], ws_recv.at[d], sibling))

    grow = rank // ncol
    gram = dot(left_t, left)
    for h in range(2):
        gpart[h] = gram[:, h * LANES : (h + 1) * LANES].reshape(ncol, grow, LANES)
    gpeers = [(d, flip) for d in range(ny) for flip in range(2) if (d, flip) != (0, 0)]
    for d, flip in gpeers:
        half = core if flip == 0 else 1 - core
        send(remote(gpart.at[half, col], ggot.at[d, flip], gy_send.at[d, flip], gy_recv.at[d, flip], at_y(d, flip)))

    value = dot(panel_t[core], buf[...])
    wpart[...] = value.reshape(ny, wrow, cols_dev)

    def merged(d):
        remote(wsibgot.at[d], wsibgot.at[d], ws_send.at[d], ws_recv.at[d], sibling).wait_recv()
        return wpart[lax.rem(y + d, ny)] + wsibgot[d].astype(F32)

    for d in sorted(range(1, ny), key=lambda d: -min(d, ny - d)):
        wsend[d] = merged(d).astype(BF16)
        send(remote(wsend.at[d], wgot.at[d], wy_send.at[d], wy_recv.at[d], at_y(d)))

    value = gpart[core, col]
    for d, flip in gpeers:
        remote(ggot.at[d, flip], ggot.at[d, flip], gy_send.at[d, flip], gy_recv.at[d, flip], at_y(d, flip)).wait_recv()
        value = value + ggot[d, flip]
    gall[core, col] = value
    slice_own = gall.at[core, col]
    for dx, dz in col_peers:
        send(remote(slice_own, slice_own, gx_send.at[dx, dz], gx_recv.at[dx, dz], at_xz(dx, dz)))
    for dx, dz in col_peers[::-1]:
        piece = gall.at[core, col_of(-dx, -dz)]
        remote(piece, piece, gx_send.at[dx, dz], gx_recv.at[dx, dz], at_xz(dx, dz)).wait_recv()
    send(remote(gall.at[core], gall.at[core], gs_send.at[0], gs_recv.at[0], sibling))
    value = merged(0)
    for d in range(1, ny):
        remote(wgot.at[d], wgot.at[d], wy_send.at[d], wy_recv.at[d], at_y(d)).wait_recv()
        value = value + wgot[d].astype(F32)
    mine = core * ny + y
    wall[mine] = value.astype(BF16)
    for d in sorted(range(1, ny), key=lambda d: -min(d, ny - d)):
        send(remote(wall.at[mine], wall.at[mine], wa_send.at[d], wa_recv.at[d], at_y(d)))
    send(remote(wall.at[mine], wall.at[mine], wf_send.at[0], wf_recv.at[0], sibling))
    remote(gall.at[1 - core], gall.at[1 - core], gs_send.at[0], gs_recv.at[0], sibling).wait_recv()
    for h in range(2):
        work[:, h * LANES : (h + 1) * LANES] = gall[h].reshape(rank, LANES)
    def forward():
        for d in near:
            piece = core * ny + lax.rem(y + ny - d, ny)
            remote(wall.at[piece], wall.at[piece], wa_send.at[d], wa_recv.at[d], at_y(d)).wait_recv()
            send(remote(wall.at[piece], wall.at[piece], wf_send.at[d], wf_recv.at[d], sibling))

    inverse_lower(work, lower_inv)
    forward()
    high, low = split(lower_inv[...])
    basis = dot_nt(left, high) + dot_nt(left, low)
    basis_low[...] = basis.astype(BF16)
    for d in range(ny):
        piece = (1 - core) * ny + lax.rem(y + ny - d, ny)
        remote(wall.at[piece], wall.at[piece], wf_send.at[d], wf_recv.at[d], sibling).wait_recv()

    together = wall[...].reshape(rank, cols_dev)
    coeff_t[...] = dot(high, together) + dot(low, together)
    squares = jnp.zeros((rank, LANES), F32)
    for i in range(cols_dev // LANES):
        value = coeff_t[:, i * LANES : (i + 1) * LANES]
        squares = squares + value * value
    value = jnp.sum(squares.T, axis=0, keepdims=True)
    nown[...] = value
    for dx, dz in col_peers:
        send(remote(nown, ngot.at[dx, dz], n_send.at[dx, dz], n_recv.at[dx, dz], at_xz(dx, dz)))
    coeff_low[...] = coeff_t[...].astype(BF16)
    begin = row * frows
    if cols_dev >= 2 * LANES:
        tile = jnp.minimum(begin // LANES, cols_dev // LANES - 2)
        near = coeff_t[:, pl.ds(pl.multiple_of(tile * LANES, LANES), 2 * LANES)]
        near = pltpu.roll(near, 2 * LANES - (begin - tile * LANES), axis=1)
    else:
        near = pltpu.roll(coeff_t[...], cols_dev - begin, axis=1)
    mine = near[:, :LANES].T[:frows]
    for copy in started:
        copy.wait_send()
    for dx, dz in col_peers[::-1]:
        got = ngot.at[dx, dz]
        remote(got, got, n_send.at[dx, dz], n_recv.at[dx, dz], at_xz(dx, dz)).wait_recv()
        value = value + ngot[dx, dz]
    inverse = 1.0 / jnp.sqrt(value + 1e-06)
    right_out[...] = mine * inverse
    scaled_out[...] = (basis * (inverse * scale)).astype(BF16)


def outputs_kernel(
    buffer, basis, scaled, coeff, right, momentum_out, update_out, right_out, momentum_low, update_low, sems, right_sem
):
    rows = momentum_low.shape[1]
    copies = [pltpu.make_async_copy(right, right_out, right_sem)]
    copies[0].start()
    for i in range(buffer.shape[0] // rows):
        here = slice(i * rows, (i + 1) * rows)
        update_low[i] = dot(scaled[here, :], coeff[...]).astype(BF16)
        copies.append(pltpu.make_async_copy(update_low.at[i], update_out.at[here], sems.at[0, i]))
        copies[-1].start()
        correction = dot(basis[here, :], coeff[...])
        momentum_low[i] = (buffer[here, :].astype(F32) - 0.05 * correction).astype(BF16)
        copies.append(pltpu.make_async_copy(momentum_low.at[i], momentum_out.at[here], sems.at[1, i]))
        copies[-1].start()
    for copy in copies:
        copy.wait()


def body(nx, momentum, gradient, right_factor):
    ny = lax.axis_size("row") // 2
    nz = lax.axis_size("col") // nx
    ncol = nx * nz
    rows_dev, cols_dev = momentum.shape
    frows, rank = right_factor.shape
    scale = math.sqrt(rows_dev * 2 * ny * cols_dev * ncol / rank)
    prow, grow, wrow = rows_dev // ncol, rank // ncol, rank // (2 * ny)
    sem = lambda *shape: pltpu.SemaphoreType.DMA(shape)
    scratch = [
        pltpu.VMEM((rows_dev, cols_dev), BF16),
        pltpu.VMEM((frows, rank), F32),
        pltpu.VMEM((2 * ny, 2 * frows, LANES), BF16),
        pltpu.VMEM((cols_dev, rank), F32),
        pltpu.VMEM((nz, prow, rank), F32),
        pltpu.VMEM((nx, nz, prow, rank), BF16),
        pltpu.VMEM((nx, nz, prow, rank), BF16),
        pltpu.VMEM((nz, prow, rank), BF16),
        pltpu.VMEM((nz, prow, rank), BF16),
        pltpu.VMEM((ncol, prow, rank), BF16),
        pltpu.VMEM((2, rank // 2, rows_dev), BF16),
        pltpu.VMEM((2, ncol, grow, LANES), F32),
        pltpu.VMEM((ny, 2, grow, LANES), F32),
        pltpu.VMEM((2, ncol, grow, LANES), F32),
        pltpu.VMEM((rank, rank), F32),
        pltpu.VMEM((rank, rank), F32),
        pltpu.VMEM((ny, wrow, cols_dev), F32),
        pltpu.VMEM((ny, wrow, cols_dev), BF16),
        pltpu.VMEM((ny, wrow, cols_dev), BF16),
        pltpu.VMEM((ny, wrow, cols_dev), BF16),
        pltpu.VMEM((ny, wrow, cols_dev), BF16),
        pltpu.VMEM((2 * ny, wrow, cols_dev), BF16),
        pltpu.VMEM((rank, cols_dev), F32),
        pltpu.VMEM((1, rank), F32),
        pltpu.VMEM((nx, nz, 1, rank), F32),
        sem(3),
        sem(ny), sem(ny), sem(ny), sem(ny),
        sem(nx, nz), sem(nx, nz), sem(nz), sem(nz), sem(nz), sem(nz), sem(nx, nz), sem(nx, nz),
        sem(ny, 2), sem(ny, 2), sem(nx, nz), sem(nx, nz), sem(1), sem(1),
        sem(ny), sem(ny), sem(ny), sem(ny), sem(ny), sem(ny), sem(ny), sem(ny),
        sem(nx, nz), sem(nx, nz),
    ]
    momentum, gradient, right_factor = [
        pltpu.with_memory_space_constraint(value, pltpu.HBM) for value in (momentum, gradient, right_factor)
    ]
    whole = pl.BlockSpec(memory_space=pltpu.VMEM)
    hbm = pl.BlockSpec(memory_space=pltpu.HBM)
    buffer, basis, scaled, coeff, new_right = pl.pallas_call(
        functools.partial(step_kernel, (ny, nx, nz, scale)),
        out_shape=[
            jax.ShapeDtypeStruct((rows_dev, cols_dev), BF16),
            jax.ShapeDtypeStruct((rows_dev, rank), BF16),
            jax.ShapeDtypeStruct((rows_dev, rank), BF16),
            jax.ShapeDtypeStruct((rank, cols_dev), BF16),
            jax.ShapeDtypeStruct((frows, rank), F32),
        ],
        in_specs=[hbm] * 3,
        out_specs=[whole] * 5,
        scratch_shapes=scratch,
        compiler_params=pltpu.CompilerParams(
            collective_id=0, has_side_effects=True, vmem_limit_bytes=48 * 1024 * 1024
        ),
        name="panel_and_factor",
    )(momentum, gradient, right_factor)
    step = min(128, rows_dev)
    return pl.pallas_call(
        outputs_kernel,
        out_shape=[jax.ShapeDtypeStruct((rows_dev, cols_dev), BF16)] * 2
        + [jax.ShapeDtypeStruct((frows, rank), F32)],
        in_specs=[whole] * 5,
        out_specs=[hbm] * 3,
        scratch_shapes=[pltpu.VMEM((rows_dev // step, step, cols_dev), BF16)] * 2
        + [sem(2, rows_dev // step), pltpu.SemaphoreType.DMA],
        compiler_params=pltpu.CompilerParams(vmem_limit_bytes=32 * 1024 * 1024),
        name="momentum_and_update",
    )(buffer, basis, scaled, coeff, new_right)


def solution(mesh, nx=X_CHIPS):
    placed = (P("row", "col"), P("row", "col"), P(("col", "row"), None))
    return jax.shard_map(
        functools.partial(body, nx), mesh=mesh, in_specs=placed, out_specs=placed, check_vma=False
    )
```

```python
import functools
import math

import jax
import jax.numpy as jnp
from jax import lax
from jax.experimental import pallas as pl
from jax.experimental.pallas import tpu as pltpu
from jax.sharding import PartitionSpec as P

MESH = pl.DeviceIdType.MESH
LANES = 128
X_CHIPS = 4
F32 = jnp.float32
BF16 = jnp.bfloat16


def dot(a, b):
    return jnp.dot(a, b, preferred_element_type=F32)


def dot_nt(a, b):
    return lax.dot_general(a, b, (((1,), (1,)), ((), ())), preferred_element_type=F32)


def split(value):
    high = value.astype(BF16)
    return high, (value - high.astype(F32)).astype(BF16)


def splat(rows, lane):
    return jnp.broadcast_to(rows[:, lane : lane + 1], (rows.shape[0], LANES))


def eliminate(block):
    n = LANES
    lanes = lax.broadcasted_iota(jnp.int32, (8, LANES), 1)
    sublane = lax.broadcasted_iota(jnp.int32, (8, LANES), 0)
    groups = [block[8 * g : 8 * g + 8, :] for g in range(n // 8)]
    for j in range(n // 8):
        base = 8 * j
        inside = (lanes >= base) & (lanes < base + 8)
        rows = [jnp.broadcast_to(groups[j][k : k + 1, :], (8, LANES)) for k in range(8)]
        entry = {(i, k): splat(rows[k], base + i) for k in range(8) for i in range(k, 8)}
        rows = [jnp.where(inside, jnp.where(lanes == base + k, 1.0, 0.0), rows[k]) for k in range(8)]
        low, inv = {}, {}
        for k in range(8):
            root = lax.rsqrt(entry[k, k])
            for i in range(k + 1, 8):
                low[i, k] = entry[i, k] * root
            for m in range(k + 1, 8):
                for i in range(m, 8):
                    entry[i, m] = entry[i, m] - low[i, k] * low[m, k]
            rows[k] = rows[k] * root
            for i in range(k + 1, 8):
                rows[i] = rows[i] - low[i, k] * rows[k]
            inv[k, k] = root
            for i in range(k):
                total = low[k, i] * inv[i, i]
                for m in range(i + 1, k):
                    total = total + low[k, m] * inv[m, i]
                inv[k, i] = -(total * root)
        value = rows[0]
        for k in range(1, 8):
            value = jnp.where(sublane == k, rows[k], value)
        groups[j] = value
        if j == n // 8 - 1:
            break
        back = []
        for i in range(8):
            terms = [inv[k, i] * rows[k] for k in range(i, 8)]
            while len(terms) > 1:
                terms = [sum(terms[a : a + 2][1:], terms[a]) for a in range(0, len(terms), 2)]
            back.append(terms[0])
        for g in range(j + 1, n // 8):
            columns = [splat(groups[g], base + k) for k in range(8)]
            terms = [columns[k] * back[k] for k in range(8)]
            while len(terms) > 1:
                terms = [terms[a] + terms[a + 1] for a in range(0, len(terms), 2)]
            groups[g] = jnp.where(inside, 0.0, groups[g]) - terms[0]
    whole = jnp.concatenate(groups, axis=0)
    at_row = lax.broadcasted_iota(jnp.int32, (n, n), 0)
    at_col = lax.broadcasted_iota(jnp.int32, (n, n), 1)
    return jnp.where(at_row >= at_col, whole, 0.0)


def exact(a, b, dims):
    return lax.dot_general(a, b, ((dims[:1], dims[1:]), ((), ())), precision=lax.Precision.HIGHEST)


def inverse_lower(work, out_ref, hook):
    top, rest = slice(0, LANES), slice(LANES, 2 * LANES)
    first = eliminate(work[top, top])
    out_ref[top, top] = first
    out_ref[top, rest] = jnp.zeros((LANES, LANES), F32)
    upper = exact(first, work[top, rest], (1, 0))
    schur = work[rest, rest] - exact(upper, upper, (0, 0))
    hook()
    second = eliminate(schur)
    out_ref[rest, rest] = second
    out_ref[rest, top] = -exact(second, exact(upper, first, (0, 0)), (1, 0))


def remote(src, dst, send, recv, device):
    return pltpu.make_async_remote_copy(
        src_ref=src, dst_ref=dst, send_sem=send, recv_sem=recv, device_id=device, device_id_type=MESH
    )


def step_kernel(
    sizes,
    momentum,
    gradient,
    factor,
    buf,
    basis_low,
    scaled_out,
    coeff_low,
    right_out,
    *scratch,
):
    ny, nx, nz, scale = sizes
    (
        grad, fown, fslot, fall, part, psend, xgot, zsend, zgot, panel, panel_t,
        gpart, ggot, gall, work, lower_inv, wpart, wsib, wsibgot, wsend, wgot, wrelay, wall, coeff_t,
        nown, ngot,
        local_sem, f_send, f_recv, fs_send, fs_recv,
        x_send, x_recv, z_send, z_recv, pz_send, pz_recv, px_send, px_recv,
        gy_send, gy_recv, gx_send, gx_recv, gs_send, gs_recv,
        ws_send, ws_recv, wy_send, wy_recv, wa_send, wa_recv, wf_send, wf_recv,
        n_send, n_recv, wr_send, wr_recv, relay_send,
    ) = scratch
    row, col = lax.axis_index("row"), lax.axis_index("col")
    y, core = row // 2, row % 2
    x, z = col // nz, col % nz
    frows, rank = factor.shape
    rows_dev, cols_dev = buf.shape
    ncol = nx * nz
    sibling = (y * 2 + 1 - core, col)

    def at_y(d, flip=0):
        core_to = core if flip == 0 else 1 - core
        return (lax.rem(y + d, ny) * 2 + core_to, col)

    def at_x(d):
        return (row, lax.rem(x + d, nx) * nz + z)

    def at_z(d):
        return (row, x * nz + lax.rem(z + d, nz))

    def col_of(dx, dz):
        return lax.rem(x + dx + nx, nx) * nz + lax.rem(z + dz + nz, nz)

    def at_xz(dx, dz):
        return (row, col_of(dx, dz))

    started, some_started = [], []

    def send(copy):
        copy.start()
        started.append(copy)

    def send_if(condition, copy):
        pl.when(condition)(lambda: copy.start())
        some_started.append((condition, copy))

    half_way = ny // 2
    relays = ny >= 4
    far_first = sorted(range(1, ny), key=lambda d: -min(d, ny - d))
    near = sorted(range(1, ny), key=lambda d: min(d, ny - d))
    if relays:
        far_first = [ny - 1] + [d for d in far_first if d != ny - 1]
        near = [ny - 1] + [d for d in near if d != ny - 1]

    def send_y(d, copy):
        if d == half_way and relays:
            send_if(core == 0, copy)
        else:
            send(copy)

    loads = [
        pltpu.make_async_copy(momentum, buf, local_sem.at[0]),
        pltpu.make_async_copy(gradient, grad, local_sem.at[1]),
        pltpu.make_async_copy(factor, fown, local_sem.at[2]),
    ]
    for copy in loads[::-1]:
        copy.start()

    peers = [at_y(d, flip) for d in range(ny) for flip in range(2) if (d, flip) != (0, 0)]
    col_peers = [(dx, dz) for dx in range(nx) for dz in range(nz) if (dx, dz) != (0, 0)]
    col_peers.sort(key=lambda d: -min(d[0], nx - d[0]) - min(d[1], nz - d[1]))
    peers += [at_xz(*d) for d in col_peers]
    barrier = pltpu.get_barrier_semaphore()
    for peer in peers:
        pl.semaphore_signal(barrier, inc=1, device_id=peer, device_id_type=MESH)
    loads[2].wait()
    fslot[row] = jnp.concatenate([fown[:, :LANES], fown[:, LANES:]], axis=0).astype(BF16)
    pl.semaphore_wait(barrier, len(peers))

    for d in far_first:
        send_y(d, remote(fslot.at[row], fslot.at[row], f_send.at[d], f_recv.at[d], at_y(d)))
    send(remote(fslot.at[row], fslot.at[row], fs_send.at[0], fs_recv.at[0], sibling))
    loads[0].wait()
    loads[1].wait()

    def add_rows(i, carry):
        here = pl.ds(pl.multiple_of(i * 32, 32), 32)
        buf[here, :] = (buf[here, :].astype(F32) + grad[here, :].astype(F32)).astype(BF16)
        return carry

    lax.fori_loop(0, rows_dev // 32, add_rows, 0)

    def unpack(source):
        whole = fslot[source].astype(F32)
        here = pl.ds(pl.multiple_of(source * frows, 8), frows)
        fall[here, :LANES] = whole[:frows]
        fall[here, LANES:] = whole[frows:]

    unpack(row)
    for d in near:
        source = lax.rem(y + ny - d, ny) * 2 + core
        remote(fslot.at[source], fslot.at[source], f_send.at[d], f_recv.at[d], at_y(ny - d)).wait_recv()
        if d == ny - 1 and relays:
            block = fslot.at[source]
            copy = remote(block, block, relay_send.at[0], f_recv.at[half_way], at_y(half_way + 1))
            send_if(core == 1, copy)
        send(remote(fslot.at[source], fslot.at[source], fs_send.at[d], fs_recv.at[d], sibling))
        unpack(source)
    for d in [0] + near:
        source = lax.rem(y + ny - d, ny) * 2 + 1 - core
        remote(fslot.at[source], fslot.at[source], fs_send.at[d], fs_recv.at[d], sibling).wait_recv()
        unpack(source)

    prow = rows_dev // ncol
    right = fall[...].astype(BF16)
    many = rows_dev // nx
    order = sorted(range(1, nz), key=lambda d: -min(d, nz - d)) + [0]
    for dx in list(range(1, nx)) + [0]:
        group = lax.rem(x + dx, nx)
        value = dot(buf[pl.ds(pl.multiple_of(group * many, many), many), :], right).reshape(nz, prow, rank)
        if dx == 0:
            part[...] = value
            continue
        psend[dx] = value.astype(BF16)
        for dz in order:
            src = psend.at[dx, lax.rem(z + dz, nz)]
            send(remote(src, xgot.at[dx, dz], x_send.at[dx, dz], x_recv.at[dx, dz], at_x(dx)))
    for dz in order:
        value = part[lax.rem(z + dz, nz)]
        for dx in range(1, nx):
            remote(xgot.at[dx, dz], xgot.at[dx, dz], x_send.at[dx, dz], x_recv.at[dx, dz], at_x(dx)).wait_recv()
            value = value + xgot[dx, dz].astype(F32)
        if dz:
            zsend[dz] = value.astype(BF16)
            send(remote(zsend.at[dz], zgot.at[dz], z_send.at[dz], z_recv.at[dz], at_z(dz)))
    for dz in sorted(range(1, nz), key=lambda d: min(d, nz - d)):
        remote(zgot.at[dz], zgot.at[dz], z_send.at[dz], z_recv.at[dz], at_z(dz)).wait_recv()
        value = value + zgot[dz].astype(F32)
    panel[col] = value.astype(BF16)
    for dz in order[:-1]:
        send(remote(panel.at[col], panel.at[col], pz_send.at[dz], pz_recv.at[dz], at_z(dz)))
    for dz in [0] + sorted(range(1, nz), key=lambda d: min(d, nz - d)):
        piece = x * nz + lax.rem(z + nz - dz, nz)
        if dz:
            remote(panel.at[piece], panel.at[piece], pz_send.at[dz], pz_recv.at[dz], at_z(dz)).wait_recv()
        for dx in range(1, nx):
            send(remote(panel.at[piece], panel.at[piece], px_send.at[dx, dz], px_recv.at[dx, dz], at_x(dx)))
    for dz in range(nz):
        for dx in range(1, nx):
            piece = lax.rem(x + nx - dx, nx) * nz + lax.rem(z + nz - dz, nz)
            remote(panel.at[piece], panel.at[piece], px_send.at[dx, dz], px_recv.at[dx, dz], at_x(dx)).wait_recv()

    left = panel[...].reshape(rows_dev, rank)
    left_t = left.T
    halves = rank // 2
    panel_t[...] = left_t.reshape(2, halves, rows_dev)

    wrow = halves // ny
    tiles = cols_dev // LANES
    cuts = [0, (tiles + 1) // 2 * LANES, cols_dev] if tiles > 1 else [0, cols_dev]
    parts = [pl.ds(a, b - a) for a, b in zip(cuts[:-1], cuts[1:])]
    for p, lot in enumerate(parts):
        value = dot(panel_t[1 - core], buf[:, lot])
        wsib[:, :, lot] = value.astype(BF16).reshape(ny, wrow, lot.size)
        src, dst = wsib.at[:, :, lot], wsibgot.at[:, :, lot]
        send(remote(src, dst, ws_send.at[p], ws_recv.at[p], sibling))

    grow = rank // ncol
    gram = dot(left_t, left)
    for h in range(2):
        gpart[h] = gram[:, h * LANES : (h + 1) * LANES].reshape(ncol, grow, LANES)
    gpeers = [(d, flip) for d in range(ny) for flip in range(2) if (d, flip) != (0, 0)]
    for d, flip in gpeers:
        half = core if flip == 0 else 1 - core
        send(remote(gpart.at[half, col], ggot.at[d, flip], gy_send.at[d, flip], gy_recv.at[d, flip], at_y(d, flip)))

    value = dot(panel_t[core], buf[...])
    wpart[...] = value.reshape(ny, wrow, cols_dev)

    def merged(d, lot):
        piece = lax.rem(y + d, ny)
        return wpart[piece, :, lot] + wsibgot[piece, :, lot].astype(F32)

    for p, lot in enumerate(parts):
        got = wsibgot.at[:, :, lot]
        remote(got, got, ws_send.at[p], ws_recv.at[p], sibling).wait_recv()
        for d in far_first:
            wsend[d, :, lot] = merged(d, lot).astype(BF16)
            src = wsend.at[d, :, lot]
            send_y(d, remote(src, wgot.at[d, :, lot], wy_send.at[d, p], wy_recv.at[d, p], at_y(d)))
            if d == half_way and relays:
                copy = remote(src, wrelay.at[:, lot], wr_send.at[p], wr_recv.at[p], at_y(ny - 1))
                send_if(core == 1, copy)

    def pass_on(p, lot):
        if not relays:
            return
        got = wrelay.at[:, lot]
        arriving = remote(got, got, wr_send.at[p], wr_recv.at[p], at_y(ny - 1))
        pl.when(core == 1)(lambda: arriving.wait_recv())
        copy = remote(got, wgot.at[half_way, :, lot], relay_send.at[1 + p], wy_recv.at[half_way, p], at_y(half_way + 1))
        send_if(core == 1, copy)

    mine = core * ny + y

    def finish(p, lot):
        value = merged(0, lot)
        for d in near:
            got = wgot.at[d, :, lot]
            remote(got, got, wy_send.at[d, p], wy_recv.at[d, p], at_y(d)).wait_recv()
            value = value + wgot[d, :, lot].astype(F32)
        wall[mine, :, lot] = value.astype(BF16)
        block = wall.at[mine, :, lot]
        for d in far_first:
            send_y(d, remote(block, block, wa_send.at[d, p], wa_recv.at[d, p], at_y(d)))

    for p, lot in enumerate(parts):
        pass_on(p, lot)
    value = gpart[core, col]
    for d, flip in gpeers:
        remote(ggot.at[d, flip], ggot.at[d, flip], gy_send.at[d, flip], gy_recv.at[d, flip], at_y(d, flip)).wait_recv()
        value = value + ggot[d, flip]
    gall[core, col] = value
    slice_own = gall.at[core, col]
    for dx, dz in col_peers:
        send(remote(slice_own, slice_own, gx_send.at[dx, dz], gx_recv.at[dx, dz], at_xz(dx, dz)))
    for p, lot in enumerate(parts[:-1]):
        finish(p, lot)
    for dx, dz in col_peers[::-1]:
        piece = gall.at[core, col_of(-dx, -dz)]
        remote(piece, piece, gx_send.at[dx, dz], gx_recv.at[dx, dz], at_xz(dx, dz)).wait_recv()
    send(remote(gall.at[core], gall.at[core], gs_send.at[0], gs_recv.at[0], sibling))
    finish(len(parts) - 1, parts[-1])
    send(remote(wall.at[mine], wall.at[mine], wf_send.at[0], wf_recv.at[0], sibling))
    remote(gall.at[1 - core], gall.at[1 - core], gs_send.at[0], gs_recv.at[0], sibling).wait_recv()
    for h in range(2):
        work[:, h * LANES : (h + 1) * LANES] = gall[h].reshape(rank, LANES)

    def arrive(d):
        piece = core * ny + lax.rem(y + ny - d, ny)
        for p, lot in enumerate(parts):
            block = wall.at[piece, :, lot]
            remote(block, block, wa_send.at[d, p], wa_recv.at[d, p], at_y(d)).wait_recv()
            if d == ny - 1 and relays:
                copy = remote(block, block, relay_send.at[3 + p], wa_recv.at[half_way, p], at_y(half_way + 1))
                send_if(core == 1, copy)
        send(remote(wall.at[piece], wall.at[piece], wf_send.at[d], wf_recv.at[d], sibling))

    def forward():
        for d in near[1:] if relays else near:
            arrive(d)

    def hook():
        if relays:
            arrive(near[0])

    inverse_lower(work, lower_inv, hook)
    forward()
    high, low = split(lower_inv[...])
    basis = dot_nt(left, high) + dot_nt(left, low)
    basis_low[...] = basis.astype(BF16)
    for d in range(ny):
        piece = (1 - core) * ny + lax.rem(y + ny - d, ny)
        remote(wall.at[piece], wall.at[piece], wf_send.at[d], wf_recv.at[d], sibling).wait_recv()

    together = wall[...].reshape(rank, cols_dev)
    coeff_t[...] = dot(high, together) + dot(low, together)
    squares = jnp.zeros((rank, LANES), F32)
    for i in range(cols_dev // LANES):
        value = coeff_t[:, i * LANES : (i + 1) * LANES]
        squares = squares + value * value
    value = jnp.sum(squares.T, axis=0, keepdims=True)
    nown[...] = value
    for dx, dz in col_peers:
        send(remote(nown, ngot.at[dx, dz], n_send.at[dx, dz], n_recv.at[dx, dz], at_xz(dx, dz)))
    coeff_low[...] = coeff_t[...].astype(BF16)
    begin = row * frows
    if cols_dev >= 2 * LANES:
        tile = jnp.minimum(begin // LANES, cols_dev // LANES - 2)
        near = coeff_t[:, pl.ds(pl.multiple_of(tile * LANES, LANES), 2 * LANES)]
        near = pltpu.roll(near, 2 * LANES - (begin - tile * LANES), axis=1)
    else:
        near = pltpu.roll(coeff_t[...], cols_dev - begin, axis=1)
    mine = near[:, :LANES].T[:frows]
    for copy in started:
        copy.wait_send()
    for condition, copy in some_started:
        pl.when(condition)(lambda copy=copy: copy.wait_send())
    for dx, dz in col_peers[::-1]:
        got = ngot.at[dx, dz]
        remote(got, got, n_send.at[dx, dz], n_recv.at[dx, dz], at_xz(dx, dz)).wait_recv()
        value = value + ngot[dx, dz]
    inverse = 1.0 / jnp.sqrt(value + 1e-06)
    right_out[...] = mine * inverse
    scaled_out[...] = (basis * (inverse * scale)).astype(BF16)


def outputs_kernel(
    buffer, basis, scaled, coeff, right, momentum_out, update_out, right_out, momentum_low, update_low, sems, right_sem
):
    rows = momentum_low.shape[1]
    copies = [pltpu.make_async_copy(right, right_out, right_sem)]
    copies[0].start()
    for i in range(buffer.shape[0] // rows):
        here = slice(i * rows, (i + 1) * rows)
        update_low[i] = dot(scaled[here, :], coeff[...]).astype(BF16)
        copies.append(pltpu.make_async_copy(update_low.at[i], update_out.at[here], sems.at[0, i]))
        copies[-1].start()
        correction = dot(basis[here, :], coeff[...])
        momentum_low[i] = (buffer[here, :].astype(F32) - 0.05 * correction).astype(BF16)
        copies.append(pltpu.make_async_copy(momentum_low.at[i], momentum_out.at[here], sems.at[1, i]))
        copies[-1].start()
    for copy in copies:
        copy.wait()


def body(nx, momentum, gradient, right_factor):
    ny = lax.axis_size("row") // 2
    nz = lax.axis_size("col") // nx
    ncol = nx * nz
    rows_dev, cols_dev = momentum.shape
    frows, rank = right_factor.shape
    scale = math.sqrt(rows_dev * 2 * ny * cols_dev * ncol / rank)
    prow, grow, wrow = rows_dev // ncol, rank // ncol, rank // (2 * ny)
    sem = lambda *shape: pltpu.SemaphoreType.DMA(shape)
    scratch = [
        pltpu.VMEM((rows_dev, cols_dev), BF16),
        pltpu.VMEM((frows, rank), F32),
        pltpu.VMEM((2 * ny, 2 * frows, LANES), BF16),
        pltpu.VMEM((cols_dev, rank), F32),
        pltpu.VMEM((nz, prow, rank), F32),
        pltpu.VMEM((nx, nz, prow, rank), BF16),
        pltpu.VMEM((nx, nz, prow, rank), BF16),
        pltpu.VMEM((nz, prow, rank), BF16),
        pltpu.VMEM((nz, prow, rank), BF16),
        pltpu.VMEM((ncol, prow, rank), BF16),
        pltpu.VMEM((2, rank // 2, rows_dev), BF16),
        pltpu.VMEM((2, ncol, grow, LANES), F32),
        pltpu.VMEM((ny, 2, grow, LANES), F32),
        pltpu.VMEM((2, ncol, grow, LANES), F32),
        pltpu.VMEM((rank, rank), F32),
        pltpu.VMEM((rank, rank), F32),
        pltpu.VMEM((ny, wrow, cols_dev), F32),
        pltpu.VMEM((ny, wrow, cols_dev), BF16),
        pltpu.VMEM((ny, wrow, cols_dev), BF16),
        pltpu.VMEM((ny, wrow, cols_dev), BF16),
        pltpu.VMEM((ny, wrow, cols_dev), BF16),
        pltpu.VMEM((wrow, cols_dev), BF16),
        pltpu.VMEM((2 * ny, wrow, cols_dev), BF16),
        pltpu.VMEM((rank, cols_dev), F32),
        pltpu.VMEM((1, rank), F32),
        pltpu.VMEM((nx, nz, 1, rank), F32),
        sem(3),
        sem(ny), sem(ny), sem(ny), sem(ny),
        sem(nx, nz), sem(nx, nz), sem(nz), sem(nz), sem(nz), sem(nz), sem(nx, nz), sem(nx, nz),
        sem(ny, 2), sem(ny, 2), sem(nx, nz), sem(nx, nz), sem(1), sem(1),
        sem(2), sem(2), sem(ny, 2), sem(ny, 2), sem(ny, 2), sem(ny, 2), sem(ny), sem(ny),
        sem(nx, nz), sem(nx, nz), sem(2), sem(2), sem(5),
    ]
    momentum, gradient, right_factor = [
        pltpu.with_memory_space_constraint(value, pltpu.HBM) for value in (momentum, gradient, right_factor)
    ]
    whole = pl.BlockSpec(memory_space=pltpu.VMEM)
    hbm = pl.BlockSpec(memory_space=pltpu.HBM)
    buffer, basis, scaled, coeff, new_right = pl.pallas_call(
        functools.partial(step_kernel, (ny, nx, nz, scale)),
        out_shape=[
            jax.ShapeDtypeStruct((rows_dev, cols_dev), BF16),
            jax.ShapeDtypeStruct((rows_dev, rank), BF16),
            jax.ShapeDtypeStruct((rows_dev, rank), BF16),
            jax.ShapeDtypeStruct((rank, cols_dev), BF16),
            jax.ShapeDtypeStruct((frows, rank), F32),
        ],
        in_specs=[hbm] * 3,
        out_specs=[whole] * 5,
        scratch_shapes=scratch,
        compiler_params=pltpu.CompilerParams(
            collective_id=0, has_side_effects=True, vmem_limit_bytes=48 * 1024 * 1024
        ),
        name="panel_and_factor",
    )(momentum, gradient, right_factor)
    step = min(128, rows_dev)
    return pl.pallas_call(
        outputs_kernel,
        out_shape=[jax.ShapeDtypeStruct((rows_dev, cols_dev), BF16)] * 2
        + [jax.ShapeDtypeStruct((frows, rank), F32)],
        in_specs=[whole] * 5,
        out_specs=[hbm] * 3,
        scratch_shapes=[pltpu.VMEM((rows_dev // step, step, cols_dev), BF16)] * 2
        + [sem(2, rows_dev // step), pltpu.SemaphoreType.DMA],
        compiler_params=pltpu.CompilerParams(vmem_limit_bytes=32 * 1024 * 1024),
        name="momentum_and_update",
    )(buffer, basis, scaled, coeff, new_right)


def solution(mesh, nx=X_CHIPS):
    placed = (P("row", "col"), P("row", "col"), P(("col", "row"), None))
    return jax.shard_map(
        functools.partial(body, nx), mesh=mesh, in_specs=placed, out_specs=placed, check_vma=False
    )
```

```python
import functools
import math

import jax
import jax.numpy as jnp
from jax import lax
from jax.experimental import pallas as pl
from jax.experimental.pallas import tpu as pltpu
from jax.sharding import PartitionSpec as P

MESH = pl.DeviceIdType.MESH
LANES = 128
X_CHIPS = 4
F32 = jnp.float32
BF16 = jnp.bfloat16


def dot(a, b):
    return jnp.dot(a, b, preferred_element_type=F32)


def dot_nt(a, b):
    return lax.dot_general(a, b, (((1,), (1,)), ((), ())), preferred_element_type=F32)


def split(value):
    high = value.astype(BF16)
    return high, (value - high.astype(F32)).astype(BF16)


def splat(rows, lane):
    return jnp.broadcast_to(rows[:, lane : lane + 1], (rows.shape[0], LANES))


def eliminate(block, hook=None):
    n = LANES
    lanes = lax.broadcasted_iota(jnp.int32, (8, LANES), 1)
    sublane = lax.broadcasted_iota(jnp.int32, (8, LANES), 0)
    groups = [block[8 * g : 8 * g + 8, :] for g in range(n // 8)]
    for j in range(n // 8):
        if hook is not None and j == n // 16:
            hook()
        base = 8 * j
        inside = (lanes >= base) & (lanes < base + 8)
        rows = [jnp.broadcast_to(groups[j][k : k + 1, :], (8, LANES)) for k in range(8)]
        entry = {(i, k): splat(rows[k], base + i) for k in range(8) for i in range(k, 8)}
        rows = [jnp.where(inside, jnp.where(lanes == base + k, 1.0, 0.0), rows[k]) for k in range(8)]
        low, inv = {}, {}
        for k in range(8):
            root = lax.rsqrt(entry[k, k])
            for i in range(k + 1, 8):
                low[i, k] = entry[i, k] * root
            for m in range(k + 1, 8):
                for i in range(m, 8):
                    entry[i, m] = entry[i, m] - low[i, k] * low[m, k]
            rows[k] = rows[k] * root
            for i in range(k + 1, 8):
                rows[i] = rows[i] - low[i, k] * rows[k]
            inv[k, k] = root
            for i in range(k):
                total = low[k, i] * inv[i, i]
                for m in range(i + 1, k):
                    total = total + low[k, m] * inv[m, i]
                inv[k, i] = -(total * root)
        value = rows[0]
        for k in range(1, 8):
            value = jnp.where(sublane == k, rows[k], value)
        groups[j] = value
        if j == n // 8 - 1:
            break
        back = []
        for i in range(8):
            terms = [inv[k, i] * rows[k] for k in range(i, 8)]
            while len(terms) > 1:
                terms = [sum(terms[a : a + 2][1:], terms[a]) for a in range(0, len(terms), 2)]
            back.append(terms[0])
        for g in range(j + 1, n // 8):
            columns = [splat(groups[g], base + k) for k in range(8)]
            terms = [columns[k] * back[k] for k in range(8)]
            while len(terms) > 1:
                terms = [terms[a] + terms[a + 1] for a in range(0, len(terms), 2)]
            groups[g] = jnp.where(inside, 0.0, groups[g]) - terms[0]
    whole = jnp.concatenate(groups, axis=0)
    at_row = lax.broadcasted_iota(jnp.int32, (n, n), 0)
    at_col = lax.broadcasted_iota(jnp.int32, (n, n), 1)
    return jnp.where(at_row >= at_col, whole, 0.0)


def exact(a, b, dims):
    a_high, a_low = split(a)
    b_high, b_low = split(b)
    product = functools.partial(
        lax.dot_general, dimension_numbers=((dims[:1], dims[1:]), ((), ())), preferred_element_type=F32
    )
    return product(a_high, b_high) + (product(a_high, b_low) + product(a_low, b_high))


def inverse_lower(work, out_ref, hook):
    top, rest = slice(0, LANES), slice(LANES, 2 * LANES)
    first = eliminate(work[top, top])
    out_ref[top, top] = first
    out_ref[top, rest] = jnp.zeros((LANES, LANES), F32)
    upper = exact(first, work[top, rest], (1, 0))
    schur = work[rest, rest] - exact(upper, upper, (0, 0))
    second = eliminate(schur, hook)
    out_ref[rest, rest] = second
    out_ref[rest, top] = -exact(second, exact(upper, first, (0, 0)), (1, 0))


def remote(src, dst, send, recv, device):
    return pltpu.make_async_remote_copy(
        src_ref=src, dst_ref=dst, send_sem=send, recv_sem=recv, device_id=device, device_id_type=MESH
    )


def step_kernel(
    sizes,
    momentum,
    gradient,
    factor,
    buf,
    basis_low,
    scaled_out,
    coeff_low,
    right_out,
    *scratch,
):
    ny, nx, nz, scale = sizes
    (
        grad, fown, fslot, fall, part, psend, xgot, zsend, zgot, panel, panel_t,
        gpart, ggot, gall, work, lower_inv, wpart, wsib, wsibgot, wsend, wgot, wall, coeff_t,
        nown, ngot,
        local_sem, f_send, f_recv, fs_send, fs_recv,
        x_send, x_recv, z_send, z_recv, pz_send, pz_recv, px_send, px_recv,
        gy_send, gy_recv, gx_send, gx_recv, gs_send, gs_recv,
        ws_send, ws_recv, wy_send, wy_recv, wa_send, wa_recv, wf_send, wf_recv,
        n_send, n_recv,
    ) = scratch
    row, col = lax.axis_index("row"), lax.axis_index("col")
    y, core = row // 2, row % 2
    x, z = col // nz, col % nz
    frows, rank = factor.shape
    rows_dev, cols_dev = buf.shape
    ncol = nx * nz
    sibling = (y * 2 + 1 - core, col)

    def at_y(d, flip=0):
        core_to = core if flip == 0 else 1 - core
        return (lax.rem(y + d, ny) * 2 + core_to, col)

    def at_x(d):
        return (row, lax.rem(x + d, nx) * nz + z)

    def at_z(d):
        return (row, x * nz + lax.rem(z + d, nz))

    def col_of(dx, dz):
        return lax.rem(x + dx + nx, nx) * nz + lax.rem(z + dz + nz, nz)

    def at_xz(dx, dz):
        return (row, col_of(dx, dz))

    started = []

    def send(copy):
        copy.start()
        started.append(copy)

    far_first = sorted(range(1, ny), key=lambda d: -min(d, ny - d))
    near = far_first[::-1]

    loads = [
        pltpu.make_async_copy(momentum, buf, local_sem.at[0]),
        pltpu.make_async_copy(gradient, grad, local_sem.at[1]),
        pltpu.make_async_copy(factor, fown, local_sem.at[2]),
    ]
    for copy in loads[::-1]:
        copy.start()

    peers = [at_y(d, flip) for d in range(ny) for flip in range(2) if (d, flip) != (0, 0)]
    col_peers = [(dx, dz) for dx in range(nx) for dz in range(nz) if (dx, dz) != (0, 0)]
    col_peers.sort(key=lambda d: -min(d[0], nx - d[0]) - min(d[1], nz - d[1]))
    peers += [at_xz(*d) for d in col_peers]
    barrier = pltpu.get_barrier_semaphore()
    for peer in peers:
        pl.semaphore_signal(barrier, inc=1, device_id=peer, device_id_type=MESH)
    loads[2].wait()
    fslot[row] = jnp.concatenate([fown[:, :LANES], fown[:, LANES:]], axis=0).astype(BF16)
    pl.semaphore_wait(barrier, len(peers))

    for d in far_first:
        send(remote(fslot.at[row], fslot.at[row], f_send.at[d], f_recv.at[d], at_y(d)))
    send(remote(fslot.at[row], fslot.at[row], fs_send.at[0], fs_recv.at[0], sibling))
    loads[0].wait()
    loads[1].wait()

    def add_rows(i, carry):
        here = pl.ds(pl.multiple_of(i * 32, 32), 32)
        buf[here, :] = (buf[here, :].astype(F32) + grad[here, :].astype(F32)).astype(BF16)
        return carry

    lax.fori_loop(0, rows_dev // 32, add_rows, 0)

    def unpack(source):
        whole = fslot[source].astype(F32)
        here = pl.ds(pl.multiple_of(source * frows, 8), frows)
        fall[here, :LANES] = whole[:frows]
        fall[here, LANES:] = whole[frows:]

    unpack(row)
    for d in near:
        source = lax.rem(y + ny - d, ny) * 2 + core
        remote(fslot.at[source], fslot.at[source], f_send.at[d], f_recv.at[d], at_y(ny - d)).wait_recv()
        send(remote(fslot.at[source], fslot.at[source], fs_send.at[d], fs_recv.at[d], sibling))
        unpack(source)
    for d in [0] + near:
        source = lax.rem(y + ny - d, ny) * 2 + 1 - core
        remote(fslot.at[source], fslot.at[source], fs_send.at[d], fs_recv.at[d], sibling).wait_recv()
        unpack(source)

    prow = rows_dev // ncol
    right = fall[...].astype(BF16)
    many = rows_dev // nx
    order = sorted(range(1, nz), key=lambda d: -min(d, nz - d)) + [0]
    for dx in list(range(1, nx)) + [0]:
        group = lax.rem(x + dx, nx)
        value = dot(buf[pl.ds(pl.multiple_of(group * many, many), many), :], right).reshape(nz, prow, rank)
        if dx == 0:
            part[...] = value
            continue
        psend[dx] = value.astype(BF16)
        for dz in order:
            src = psend.at[dx, lax.rem(z + dz, nz)]
            send(remote(src, xgot.at[dx, dz], x_send.at[dx, dz], x_recv.at[dx, dz], at_x(dx)))
    for dz in order:
        value = part[lax.rem(z + dz, nz)]
        for dx in range(1, nx):
            remote(xgot.at[dx, dz], xgot.at[dx, dz], x_send.at[dx, dz], x_recv.at[dx, dz], at_x(dx)).wait_recv()
            value = value + xgot[dx, dz].astype(F32)
        if dz:
            zsend[dz] = value.astype(BF16)
            send(remote(zsend.at[dz], zgot.at[dz], z_send.at[dz], z_recv.at[dz], at_z(dz)))
    for dz in sorted(range(1, nz), key=lambda d: min(d, nz - d)):
        remote(zgot.at[dz], zgot.at[dz], z_send.at[dz], z_recv.at[dz], at_z(dz)).wait_recv()
        value = value + zgot[dz].astype(F32)
    panel[col] = value.astype(BF16)
    for dz in order[:-1]:
        send(remote(panel.at[col], panel.at[col], pz_send.at[dz], pz_recv.at[dz], at_z(dz)))
    for dz in [0] + sorted(range(1, nz), key=lambda d: min(d, nz - d)):
        piece = x * nz + lax.rem(z + nz - dz, nz)
        if dz:
            remote(panel.at[piece], panel.at[piece], pz_send.at[dz], pz_recv.at[dz], at_z(dz)).wait_recv()
        for dx in range(1, nx):
            send(remote(panel.at[piece], panel.at[piece], px_send.at[dx, dz], px_recv.at[dx, dz], at_x(dx)))
    for dz in range(nz):
        for dx in range(1, nx):
            piece = lax.rem(x + nx - dx, nx) * nz + lax.rem(z + nz - dz, nz)
            remote(panel.at[piece], panel.at[piece], px_send.at[dx, dz], px_recv.at[dx, dz], at_x(dx)).wait_recv()

    left = panel[...].reshape(rows_dev, rank)
    left_t = left.T
    halves = rank // 2
    panel_t[...] = left_t.reshape(2, halves, rows_dev)

    grow = rank // ncol
    gram = dot(left_t, left)
    for h in range(2):
        gpart[h] = gram[:, h * LANES : (h + 1) * LANES].reshape(ncol, grow, LANES)
    gpeers = [(d, flip) for d in range(ny) for flip in range(2) if (d, flip) != (0, 0)]
    for d, flip in gpeers:
        half = core if flip == 0 else 1 - core
        send(remote(gpart.at[half, col], ggot.at[d, flip], gy_send.at[d, flip], gy_recv.at[d, flip], at_y(d, flip)))

    wrow = halves // ny
    tiles = cols_dev // LANES
    cuts = [0, (tiles + 1) // 2 * LANES, cols_dev] if tiles > 1 else [0, cols_dev]
    parts = [pl.ds(a, b - a) for a, b in zip(cuts[:-1], cuts[1:])]
    for p, lot in enumerate(parts):
        value = dot(panel_t[1 - core], buf[:, lot])
        wsib[:, :, lot] = value.astype(BF16).reshape(ny, wrow, lot.size)
        src, dst = wsib.at[:, :, lot], wsibgot.at[:, :, lot]
        send(remote(src, dst, ws_send.at[p], ws_recv.at[p], sibling))

    value = dot(panel_t[core], buf[...])
    wpart[...] = value.reshape(ny, wrow, cols_dev)

    def merged(d, lot):
        piece = lax.rem(y + d, ny)
        return wpart[piece, :, lot] + wsibgot[piece, :, lot].astype(F32)

    def spread(p, lot):
        got = wsibgot.at[:, :, lot]
        remote(got, got, ws_send.at[p], ws_recv.at[p], sibling).wait_recv()
        for d in far_first:
            wsend[d, :, lot] = merged(d, lot).astype(BF16)
            src = wsend.at[d, :, lot]
            send(remote(src, wgot.at[d, :, lot], wy_send.at[d, p], wy_recv.at[d, p], at_y(d)))

    mine = core * ny + y

    def finish(p, lot):
        value = merged(0, lot)
        for d in near:
            got = wgot.at[d, :, lot]
            remote(got, got, wy_send.at[d, p], wy_recv.at[d, p], at_y(d)).wait_recv()
            value = value + wgot[d, :, lot].astype(F32)
        wall[mine, :, lot] = value.astype(BF16)
        block = wall.at[mine, :, lot]
        for d in far_first:
            send(remote(block, block, wa_send.at[d, p], wa_recv.at[d, p], at_y(d)))

    spread(0, parts[0])
    value = gpart[core, col]
    for d, flip in gpeers:
        remote(ggot.at[d, flip], ggot.at[d, flip], gy_send.at[d, flip], gy_recv.at[d, flip], at_y(d, flip)).wait_recv()
        value = value + ggot[d, flip]
    gall[core, col] = value
    slice_own = gall.at[core, col]
    for dx, dz in col_peers:
        send(remote(slice_own, slice_own, gx_send.at[dx, dz], gx_recv.at[dx, dz], at_xz(dx, dz)))
    for p, lot in enumerate(parts[1:]):
        spread(p + 1, lot)
    for p, lot in enumerate(parts[:-1]):
        finish(p, lot)
    for dx, dz in col_peers[::-1]:
        piece = gall.at[core, col_of(-dx, -dz)]
        remote(piece, piece, gx_send.at[dx, dz], gx_recv.at[dx, dz], at_xz(dx, dz)).wait_recv()
    send(remote(gall.at[core], gall.at[core], gs_send.at[0], gs_recv.at[0], sibling))
    finish(len(parts) - 1, parts[-1])
    send(remote(wall.at[mine], wall.at[mine], wf_send.at[0], wf_recv.at[0], sibling))
    remote(gall.at[1 - core], gall.at[1 - core], gs_send.at[0], gs_recv.at[0], sibling).wait_recv()
    for h in range(2):
        work[:, h * LANES : (h + 1) * LANES] = gall[h].reshape(rank, LANES)

    def arrive(d):
        piece = core * ny + lax.rem(y + ny - d, ny)
        for p, lot in enumerate(parts):
            block = wall.at[piece, :, lot]
            remote(block, block, wa_send.at[d, p], wa_recv.at[d, p], at_y(d)).wait_recv()
        send(remote(wall.at[piece], wall.at[piece], wf_send.at[d], wf_recv.at[d], sibling))

    def forward():
        for d in near:
            arrive(d)

    inverse_lower(work, lower_inv, forward)
    high, low = split(lower_inv[...])
    for d in range(ny):
        piece = (1 - core) * ny + lax.rem(y + ny - d, ny)
        remote(wall.at[piece], wall.at[piece], wf_send.at[d], wf_recv.at[d], sibling).wait_recv()

    together = wall[...].reshape(rank, cols_dev)
    coeff_t[...] = dot(high, together) + dot(low, together)
    squares = jnp.zeros((rank, LANES), F32)
    for i in range(cols_dev // LANES):
        value = coeff_t[:, i * LANES : (i + 1) * LANES]
        squares = squares + value * value
    value = jnp.sum(squares.T, axis=0, keepdims=True)
    nown[...] = value
    for dx, dz in col_peers:
        send(remote(nown, ngot.at[dx, dz], n_send.at[dx, dz], n_recv.at[dx, dz], at_xz(dx, dz)))
    coeff_low[...] = coeff_t[...].astype(BF16)
    basis = dot_nt(left, high) + dot_nt(left, low)
    basis_low[...] = basis.astype(BF16)
    begin = row * frows
    if cols_dev >= 2 * LANES:
        tile = jnp.minimum(begin // LANES, cols_dev // LANES - 2)
        near = coeff_t[:, pl.ds(pl.multiple_of(tile * LANES, LANES), 2 * LANES)]
        near = pltpu.roll(near, 2 * LANES - (begin - tile * LANES), axis=1)
    else:
        near = pltpu.roll(coeff_t[...], cols_dev - begin, axis=1)
    mine = near[:, :LANES].T[:frows]
    for copy in started:
        copy.wait_send()
    for dx, dz in col_peers[::-1]:
        got = ngot.at[dx, dz]
        remote(got, got, n_send.at[dx, dz], n_recv.at[dx, dz], at_xz(dx, dz)).wait_recv()
        value = value + ngot[dx, dz]
    inverse = 1.0 / jnp.sqrt(value + 1e-06)
    right_out[...] = mine * inverse
    scaled_out[...] = (basis * (inverse * scale)).astype(BF16)


def outputs_kernel(
    buffer, basis, scaled, coeff, right, momentum_out, update_out, right_out, momentum_low, update_low, sems, right_sem
):
    rows = momentum_low.shape[1]
    copies = [pltpu.make_async_copy(right, right_out, right_sem)]
    copies[0].start()
    for i in range(buffer.shape[0] // rows):
        here = slice(i * rows, (i + 1) * rows)
        update_low[i] = dot(scaled[here, :], coeff[...]).astype(BF16)
        copies.append(pltpu.make_async_copy(update_low.at[i], update_out.at[here], sems.at[0, i]))
        copies[-1].start()
        correction = dot(basis[here, :], coeff[...])
        momentum_low[i] = (buffer[here, :].astype(F32) - 0.05 * correction).astype(BF16)
        copies.append(pltpu.make_async_copy(momentum_low.at[i], momentum_out.at[here], sems.at[1, i]))
        copies[-1].start()
    for copy in copies:
        copy.wait()


def body(nx, momentum, gradient, right_factor):
    ny = lax.axis_size("row") // 2
    nz = lax.axis_size("col") // nx
    ncol = nx * nz
    rows_dev, cols_dev = momentum.shape
    frows, rank = right_factor.shape
    scale = math.sqrt(rows_dev * 2 * ny * cols_dev * ncol / rank)
    prow, grow, wrow = rows_dev // ncol, rank // ncol, rank // (2 * ny)
    sem = lambda *shape: pltpu.SemaphoreType.DMA(shape)
    scratch = [
        pltpu.VMEM((rows_dev, cols_dev), BF16),
        pltpu.VMEM((frows, rank), F32),
        pltpu.VMEM((2 * ny, 2 * frows, LANES), BF16),
        pltpu.VMEM((cols_dev, rank), F32),
        pltpu.VMEM((nz, prow, rank), F32),
        pltpu.VMEM((nx, nz, prow, rank), BF16),
        pltpu.VMEM((nx, nz, prow, rank), BF16),
        pltpu.VMEM((nz, prow, rank), BF16),
        pltpu.VMEM((nz, prow, rank), BF16),
        pltpu.VMEM((ncol, prow, rank), BF16),
        pltpu.VMEM((2, rank // 2, rows_dev), BF16),
        pltpu.VMEM((2, ncol, grow, LANES), F32),
        pltpu.VMEM((ny, 2, grow, LANES), F32),
        pltpu.VMEM((2, ncol, grow, LANES), F32),
        pltpu.VMEM((rank, rank), F32),
        pltpu.VMEM((rank, rank), F32),
        pltpu.VMEM((ny, wrow, cols_dev), F32),
        pltpu.VMEM((ny, wrow, cols_dev), BF16),
        pltpu.VMEM((ny, wrow, cols_dev), BF16),
        pltpu.VMEM((ny, wrow, cols_dev), BF16),
        pltpu.VMEM((ny, wrow, cols_dev), BF16),
        pltpu.VMEM((2 * ny, wrow, cols_dev), BF16),
        pltpu.VMEM((rank, cols_dev), F32),
        pltpu.VMEM((1, rank), F32),
        pltpu.VMEM((nx, nz, 1, rank), F32),
        sem(3),
        sem(ny), sem(ny), sem(ny), sem(ny),
        sem(nx, nz), sem(nx, nz), sem(nz), sem(nz), sem(nz), sem(nz), sem(nx, nz), sem(nx, nz),
        sem(ny, 2), sem(ny, 2), sem(nx, nz), sem(nx, nz), sem(1), sem(1),
        sem(2), sem(2), sem(ny, 2), sem(ny, 2), sem(ny, 2), sem(ny, 2), sem(ny), sem(ny),
        sem(nx, nz), sem(nx, nz),
    ]
    momentum, gradient, right_factor = [
        pltpu.with_memory_space_constraint(value, pltpu.HBM) for value in (momentum, gradient, right_factor)
    ]
    whole = pl.BlockSpec(memory_space=pltpu.VMEM)
    hbm = pl.BlockSpec(memory_space=pltpu.HBM)
    buffer, basis, scaled, coeff, new_right = pl.pallas_call(
        functools.partial(step_kernel, (ny, nx, nz, scale)),
        out_shape=[
            jax.ShapeDtypeStruct((rows_dev, cols_dev), BF16),
            jax.ShapeDtypeStruct((rows_dev, rank), BF16),
            jax.ShapeDtypeStruct((rows_dev, rank), BF16),
            jax.ShapeDtypeStruct((rank, cols_dev), BF16),
            jax.ShapeDtypeStruct((frows, rank), F32),
        ],
        in_specs=[hbm] * 3,
        out_specs=[whole] * 5,
        scratch_shapes=scratch,
        compiler_params=pltpu.CompilerParams(
            collective_id=0, has_side_effects=True, vmem_limit_bytes=48 * 1024 * 1024
        ),
        name="panel_and_factor",
    )(momentum, gradient, right_factor)
    step = min(128, rows_dev)
    return pl.pallas_call(
        outputs_kernel,
        out_shape=[jax.ShapeDtypeStruct((rows_dev, cols_dev), BF16)] * 2
        + [jax.ShapeDtypeStruct((frows, rank), F32)],
        in_specs=[whole] * 5,
        out_specs=[hbm] * 3,
        scratch_shapes=[pltpu.VMEM((rows_dev // step, step, cols_dev), BF16)] * 2
        + [sem(2, rows_dev // step), pltpu.SemaphoreType.DMA],
        compiler_params=pltpu.CompilerParams(vmem_limit_bytes=32 * 1024 * 1024),
        name="momentum_and_update",
    )(buffer, basis, scaled, coeff, new_right)


def solution(mesh, nx=X_CHIPS):
    placed = (P("row", "col"), P("row", "col"), P(("col", "row"), None))
    return jax.shard_map(
        functools.partial(body, nx), mesh=mesh, in_specs=placed, out_specs=placed, check_vma=False
    )
```

```python
import functools
import math

import jax
import jax.numpy as jnp
from jax import lax
from jax.experimental import pallas as pl
from jax.experimental.pallas import tpu as pltpu
from jax.sharding import PartitionSpec as P

MESH = pl.DeviceIdType.MESH
LANES = 128
X_CHIPS = 4
F32 = jnp.float32
BF16 = jnp.bfloat16


def dot(a, b):
    return jnp.dot(a, b, preferred_element_type=F32)


def dot_nt(a, b):
    return lax.dot_general(a, b, (((1,), (1,)), ((), ())), preferred_element_type=F32)


def split(value):
    high = value.astype(BF16)
    return high, (value - high.astype(F32)).astype(BF16)


def splat(rows, lane):
    return jnp.broadcast_to(rows[:, lane : lane + 1], (rows.shape[0], LANES))


def eliminate(block, hooks):
    n = LANES
    lanes = lax.broadcasted_iota(jnp.int32, (8, LANES), 1)
    sublane = lax.broadcasted_iota(jnp.int32, (8, LANES), 0)
    groups = [block[8 * g : 8 * g + 8, :] for g in range(n // 8)]
    for j in range(n // 8):
        if j in hooks:
            hooks[j]()
        base = 8 * j
        inside = (lanes >= base) & (lanes < base + 8)
        rows = [jnp.broadcast_to(groups[j][k : k + 1, :], (8, LANES)) for k in range(8)]
        entry = {(i, k): splat(rows[k], base + i) for k in range(8) for i in range(k, 8)}
        rows = [jnp.where(inside, jnp.where(lanes == base + k, 1.0, 0.0), rows[k]) for k in range(8)]
        low, inv = {}, {}
        for k in range(8):
            root = lax.rsqrt(entry[k, k])
            for i in range(k + 1, 8):
                low[i, k] = entry[i, k] * root
            for m in range(k + 1, 8):
                for i in range(m, 8):
                    entry[i, m] = entry[i, m] - low[i, k] * low[m, k]
            rows[k] = rows[k] * root
            for i in range(k + 1, 8):
                rows[i] = rows[i] - low[i, k] * rows[k]
            inv[k, k] = root
            for i in range(k):
                total = low[k, i] * inv[i, i]
                for m in range(i + 1, k):
                    total = total + low[k, m] * inv[m, i]
                inv[k, i] = -(total * root)
        value = rows[0]
        for k in range(1, 8):
            value = jnp.where(sublane == k, rows[k], value)
        groups[j] = value
        if j == n // 8 - 1:
            break
        back = []
        for i in range(8):
            terms = [inv[k, i] * rows[k] for k in range(i, 8)]
            while len(terms) > 1:
                terms = [sum(terms[a : a + 2][1:], terms[a]) for a in range(0, len(terms), 2)]
            back.append(terms[0])
        for g in range(j + 1, n // 8):
            columns = [splat(groups[g], base + k) for k in range(8)]
            terms = [columns[k] * back[k] for k in range(8)]
            while len(terms) > 1:
                terms = [terms[a] + terms[a + 1] for a in range(0, len(terms), 2)]
            groups[g] = jnp.where(inside, 0.0, groups[g]) - terms[0]
    whole = jnp.concatenate(groups, axis=0)
    at_row = lax.broadcasted_iota(jnp.int32, (n, n), 0)
    at_col = lax.broadcasted_iota(jnp.int32, (n, n), 1)
    return jnp.where(at_row >= at_col, whole, 0.0)


def exact(a, b, dims):
    a_high, a_low = split(a)
    b_high, b_low = split(b)
    product = functools.partial(
        lax.dot_general, dimension_numbers=((dims[:1], dims[1:]), ((), ())), preferred_element_type=F32
    )
    return product(a_high, b_high) + (product(a_high, b_low) + product(a_low, b_high))


def inverse_lower(leading, rest, out_ref, early, late):
    top, bottom = slice(0, LANES), slice(LANES, 2 * LANES)
    first = eliminate(leading, {2: early})
    out_ref[top, top] = first
    out_ref[top, bottom] = jnp.zeros((LANES, LANES), F32)
    across, trailing = rest()
    upper = exact(first, across, (1, 1))
    second = eliminate(trailing - exact(upper, upper, (0, 0)), {LANES // 16: late})
    out_ref[bottom, bottom] = second
    out_ref[bottom, top] = -exact(second, exact(upper, first, (0, 0)), (1, 0))


def remote(src, dst, send, recv, device):
    return pltpu.make_async_remote_copy(
        src_ref=src, dst_ref=dst, send_sem=send, recv_sem=recv, device_id=device, device_id_type=MESH
    )


def step_kernel(
    sizes,
    momentum,
    gradient,
    factor,
    buf,
    basis_low,
    scaled_out,
    coeff_low,
    right_out,
    *scratch,
):
    ny, nx, nz, scale = sizes
    (
        grad, fown, fslot, fall, part, psend, xgot, zsend, zgot, panel,
        gpart, ggot, gall, lower_inv, wpart, wsib, wsibgot, wsend, wgot, wall, coeff_t,
        nown, ngot,
        local_sem, f_send, f_recv, fs_send, fs_recv,
        x_send, x_recv, z_send, z_recv, pz_send, pz_recv, px_send, px_recv,
        gy_send, gy_recv, gx_send, gx_recv, gs_send, gs_recv,
        ws_send, ws_recv, wy_send, wy_recv, wa_send, wa_recv, wf_send, wf_recv,
        n_send, n_recv,
    ) = scratch
    row, col = lax.axis_index("row"), lax.axis_index("col")
    y, core = row // 2, row % 2
    x, z = col // nz, col % nz
    frows, rank = factor.shape
    rows_dev, cols_dev = buf.shape
    ncol = nx * nz
    sibling = (y * 2 + 1 - core, col)

    def at_y(d, flip=0):
        core_to = core if flip == 0 else 1 - core
        return (lax.rem(y + d, ny) * 2 + core_to, col)

    def at_x(d):
        return (row, lax.rem(x + d, nx) * nz + z)

    def at_z(d):
        return (row, x * nz + lax.rem(z + d, nz))

    def col_of(dx, dz):
        return lax.rem(x + dx + nx, nx) * nz + lax.rem(z + dz + nz, nz)

    def at_xz(dx, dz):
        return (row, col_of(dx, dz))

    started = []

    def send(copy):
        copy.start()
        started.append(copy)

    far_first = sorted(range(1, ny), key=lambda d: -min(d, ny - d))
    near = far_first[::-1]

    loads = [
        pltpu.make_async_copy(momentum, buf, local_sem.at[0]),
        pltpu.make_async_copy(gradient, grad, local_sem.at[1]),
        pltpu.make_async_copy(factor, fown, local_sem.at[2]),
    ]
    for copy in loads[::-1]:
        copy.start()

    peers = [at_y(d, flip) for d in range(ny) for flip in range(2) if (d, flip) != (0, 0)]
    col_peers = [(dx, dz) for dx in range(nx) for dz in range(nz) if (dx, dz) != (0, 0)]
    col_peers.sort(key=lambda d: -min(d[0], nx - d[0]) - min(d[1], nz - d[1]))
    peers += [at_xz(*d) for d in col_peers]
    barrier = pltpu.get_barrier_semaphore()
    for peer in peers:
        pl.semaphore_signal(barrier, inc=1, device_id=peer, device_id_type=MESH)
    loads[2].wait()
    fslot[row] = jnp.concatenate([fown[:, :LANES], fown[:, LANES:]], axis=0).astype(BF16)
    pl.semaphore_wait(barrier, len(peers))

    for d in far_first:
        send(remote(fslot.at[row], fslot.at[row], f_send.at[d], f_recv.at[d], at_y(d)))
    send(remote(fslot.at[row], fslot.at[row], fs_send.at[0], fs_recv.at[0], sibling))
    loads[0].wait()
    loads[1].wait()

    def add_rows(i, carry):
        here = pl.ds(pl.multiple_of(i * 32, 32), 32)
        buf[here, :] = (buf[here, :].astype(F32) + grad[here, :].astype(F32)).astype(BF16)
        return carry

    lax.fori_loop(0, rows_dev // 32, add_rows, 0)

    def unpack(source):
        whole = fslot[source].astype(F32)
        here = pl.ds(pl.multiple_of(source * frows, 8), frows)
        fall[here, :LANES] = whole[:frows]
        fall[here, LANES:] = whole[frows:]

    unpack(row)
    for d in near:
        source = lax.rem(y + ny - d, ny) * 2 + core
        remote(fslot.at[source], fslot.at[source], f_send.at[d], f_recv.at[d], at_y(ny - d)).wait_recv()
        send(remote(fslot.at[source], fslot.at[source], fs_send.at[d], fs_recv.at[d], sibling))
        unpack(source)
    for d in [0] + near:
        source = lax.rem(y + ny - d, ny) * 2 + 1 - core
        remote(fslot.at[source], fslot.at[source], fs_send.at[d], fs_recv.at[d], sibling).wait_recv()
        unpack(source)

    prow = rows_dev // ncol
    right = fall[...].astype(BF16)
    many = rows_dev // nx
    order = sorted(range(1, nz), key=lambda d: -min(d, nz - d)) + [0]
    for dx in list(range(1, nx)) + [0]:
        group = lax.rem(x + dx, nx)
        value = dot(buf[pl.ds(pl.multiple_of(group * many, many), many), :], right).reshape(nz, prow, rank)
        if dx == 0:
            part[...] = value
            continue
        psend[dx] = value.astype(BF16)
        for dz in order:
            src = psend.at[dx, lax.rem(z + dz, nz)]
            send(remote(src, xgot.at[dx, dz], x_send.at[dx, dz], x_recv.at[dx, dz], at_x(dx)))
    for dz in order:
        value = part[lax.rem(z + dz, nz)]
        for dx in range(1, nx):
            remote(xgot.at[dx, dz], xgot.at[dx, dz], x_send.at[dx, dz], x_recv.at[dx, dz], at_x(dx)).wait_recv()
            value = value + xgot[dx, dz].astype(F32)
        if dz:
            zsend[dz] = value.astype(BF16)
            send(remote(zsend.at[dz], zgot.at[dz], z_send.at[dz], z_recv.at[dz], at_z(dz)))
    for dz in sorted(range(1, nz), key=lambda d: min(d, nz - d)):
        remote(zgot.at[dz], zgot.at[dz], z_send.at[dz], z_recv.at[dz], at_z(dz)).wait_recv()
        value = value + zgot[dz].astype(F32)
    panel[col] = value.astype(BF16)
    for dz in order[:-1]:
        send(remote(panel.at[col], panel.at[col], pz_send.at[dz], pz_recv.at[dz], at_z(dz)))
    for dz in [0] + sorted(range(1, nz), key=lambda d: min(d, nz - d)):
        piece = x * nz + lax.rem(z + nz - dz, nz)
        if dz:
            remote(panel.at[piece], panel.at[piece], pz_send.at[dz], pz_recv.at[dz], at_z(dz)).wait_recv()
        for dx in range(1, nx):
            send(remote(panel.at[piece], panel.at[piece], px_send.at[dx, dz], px_recv.at[dx, dz], at_x(dx)))
    for dz in range(nz):
        for dx in range(1, nx):
            piece = lax.rem(x + nx - dx, nx) * nz + lax.rem(z + nz - dz, nz)
            remote(panel.at[piece], panel.at[piece], px_send.at[dx, dz], px_recv.at[dx, dz], at_x(dx)).wait_recv()

    left = panel[...].reshape(rows_dev, rank)
    left_t = left.T
    halves = rank // 2

    grow = rank // ncol
    gram = dot(left_t, left)
    for h in range(2):
        gpart[h] = gram[:, h * LANES : (h + 1) * LANES].reshape(ncol, grow, LANES)
    gpeers = [(d, flip) for d in range(ny) for flip in range(2) if (d, flip) != (0, 0)]
    own_half = jnp.where(col < ncol // 2, 0, core)
    for d, flip in gpeers:
        half = own_half if flip == 0 else jnp.where(col < ncol // 2, 0, 1 - core)
        send(remote(gpart.at[half, col], ggot.at[d, flip], gy_send.at[d, flip], gy_recv.at[d, flip], at_y(d, flip)))

    wrow = halves // ny
    tiles = cols_dev // LANES
    cuts = [0, (tiles + 1) // 2 * LANES, cols_dev] if tiles > 1 else [0, cols_dev]
    parts = [pl.ds(a, b - a) for a, b in zip(cuts[:-1], cuts[1:])]
    for p, lot in enumerate(parts):
        wpart[:, :, :, lot] = dot(left_t, buf[:, lot]).reshape(2, ny, wrow, lot.size)
        wsib[:, :, lot] = wpart[1 - core, :, :, lot].astype(BF16)
        src, dst = wsib.at[:, :, lot], wsibgot.at[:, :, lot]
        send(remote(src, dst, ws_send.at[p], ws_recv.at[p], sibling))

    def merged(d, lot):
        piece = lax.rem(y + d, ny)
        return wpart[core, piece, :, lot] + wsibgot[piece, :, lot].astype(F32)

    def spread(p, lot):
        got = wsibgot.at[:, :, lot]
        remote(got, got, ws_send.at[p], ws_recv.at[p], sibling).wait_recv()
        for d in far_first:
            wsend[d, :, lot] = merged(d, lot).astype(BF16)
            src = wsend.at[d, :, lot]
            send(remote(src, wgot.at[d, :, lot], wy_send.at[d, p], wy_recv.at[d, p], at_y(d)))

    mine = core * ny + y

    def finish(p, lot):
        value = merged(0, lot)
        for d in near:
            got = wgot.at[d, :, lot]
            remote(got, got, wy_send.at[d, p], wy_recv.at[d, p], at_y(d)).wait_recv()
            value = value + wgot[d, :, lot].astype(F32)
        wall[mine, :, lot] = value.astype(BF16)
        block = wall.at[mine, :, lot]
        for d in far_first:
            send(remote(block, block, wa_send.at[d, p], wa_recv.at[d, p], at_y(d)))

    spread(0, parts[0])
    value = gpart[own_half, col]
    for d, flip in gpeers:
        remote(ggot.at[d, flip], ggot.at[d, flip], gy_send.at[d, flip], gy_recv.at[d, flip], at_y(d, flip)).wait_recv()
        value = value + ggot[d, flip]
    gall[core, col] = value
    slice_own = gall.at[core, col]
    for dx, dz in col_peers:
        send(remote(slice_own, slice_own, gx_send.at[dx, dz], gx_recv.at[dx, dz], at_xz(dx, dz)))
    for p, lot in enumerate(parts[1:]):
        spread(p + 1, lot)
    for p, lot in enumerate(parts[:-1]):
        finish(p, lot)
    for dx, dz in col_peers[::-1]:
        piece = gall.at[core, col_of(-dx, -dz)]
        remote(piece, piece, gx_send.at[dx, dz], gx_recv.at[dx, dz], at_xz(dx, dz)).wait_recv()
    lower_rows = pl.ds(ncol // 2, ncol // 2)
    ours, theirs = gall.at[core, lower_rows], gall.at[1 - core, lower_rows]
    send(remote(ours, ours, gs_send.at[0], gs_recv.at[0], sibling))

    def rest():
        remote(theirs, theirs, gs_send.at[0], gs_recv.at[0], sibling).wait_recv()
        return [gall[h, lower_rows].reshape(LANES, LANES) for h in range(2)]

    def finish_last():
        finish(len(parts) - 1, parts[-1])
        send(remote(wall.at[mine], wall.at[mine], wf_send.at[0], wf_recv.at[0], sibling))

    def arrive(d):
        piece = core * ny + lax.rem(y + ny - d, ny)
        for p, lot in enumerate(parts):
            block = wall.at[piece, :, lot]
            remote(block, block, wa_send.at[d, p], wa_recv.at[d, p], at_y(d)).wait_recv()
        send(remote(wall.at[piece], wall.at[piece], wf_send.at[d], wf_recv.at[d], sibling))

    def forward():
        for d in near:
            arrive(d)

    leading = gall[core, pl.ds(0, ncol // 2)].reshape(LANES, LANES)
    inverse_lower(leading, rest, lower_inv, finish_last, forward)
    high, low = split(lower_inv[...])
    for d in range(ny):
        piece = (1 - core) * ny + lax.rem(y + ny - d, ny)
        remote(wall.at[piece], wall.at[piece], wf_send.at[d], wf_recv.at[d], sibling).wait_recv()

    together = wall[...].reshape(rank, cols_dev)
    both = dot(jnp.concatenate([high, low], axis=0), together)
    coeff_t[...] = both[:rank] + both[rank:]
    squares = jnp.zeros((rank, LANES), F32)
    for i in range(cols_dev // LANES):
        value = coeff_t[:, i * LANES : (i + 1) * LANES]
        squares = squares + value * value
    value = jnp.sum(squares.T, axis=0, keepdims=True)
    nown[...] = value
    for dx, dz in col_peers:
        send(remote(nown, ngot.at[dx, dz], n_send.at[dx, dz], n_recv.at[dx, dz], at_xz(dx, dz)))
    coeff_low[...] = coeff_t[...].astype(BF16)
    basis = dot_nt(left, high) + dot_nt(left, low)
    basis_low[...] = basis.astype(BF16)
    begin = row * frows
    if cols_dev >= 2 * LANES:
        tile = jnp.minimum(begin // LANES, cols_dev // LANES - 2)
        near = coeff_t[:, pl.ds(pl.multiple_of(tile * LANES, LANES), 2 * LANES)]
        near = pltpu.roll(near, 2 * LANES - (begin - tile * LANES), axis=1)
    else:
        near = pltpu.roll(coeff_t[...], cols_dev - begin, axis=1)
    mine = near[:, :LANES].T[:frows]
    for copy in started:
        copy.wait_send()
    for dx, dz in col_peers[::-1]:
        got = ngot.at[dx, dz]
        remote(got, got, n_send.at[dx, dz], n_recv.at[dx, dz], at_xz(dx, dz)).wait_recv()
        value = value + ngot[dx, dz]
    inverse = 1.0 / jnp.sqrt(value + 1e-06)
    right_out[...] = mine * inverse
    scaled_out[...] = (basis * (inverse * scale)).astype(BF16)


def outputs_kernel(
    buffer, basis, scaled, coeff, right, momentum_out, update_out, right_out, momentum_low, update_low, sems, right_sem
):
    rows = momentum_low.shape[1]
    copies = [pltpu.make_async_copy(right, right_out, right_sem)]
    copies[0].start()
    for i in range(buffer.shape[0] // rows):
        here = slice(i * rows, (i + 1) * rows)
        update_low[i] = dot(scaled[here, :], coeff[...]).astype(BF16)
        copies.append(pltpu.make_async_copy(update_low.at[i], update_out.at[here], sems.at[0, i]))
        copies[-1].start()
        correction = dot(basis[here, :], coeff[...])
        momentum_low[i] = (buffer[here, :].astype(F32) - 0.05 * correction).astype(BF16)
        copies.append(pltpu.make_async_copy(momentum_low.at[i], momentum_out.at[here], sems.at[1, i]))
        copies[-1].start()
    for copy in copies:
        copy.wait()


def body(nx, momentum, gradient, right_factor):
    ny = lax.axis_size("row") // 2
    nz = lax.axis_size("col") // nx
    ncol = nx * nz
    rows_dev, cols_dev = momentum.shape
    frows, rank = right_factor.shape
    scale = math.sqrt(rows_dev * 2 * ny * cols_dev * ncol / rank)
    prow, grow, wrow = rows_dev // ncol, rank // ncol, rank // (2 * ny)
    sem = lambda *shape: pltpu.SemaphoreType.DMA(shape)
    scratch = [
        pltpu.VMEM((rows_dev, cols_dev), BF16),
        pltpu.VMEM((frows, rank), F32),
        pltpu.VMEM((2 * ny, 2 * frows, LANES), BF16),
        pltpu.VMEM((cols_dev, rank), F32),
        pltpu.VMEM((nz, prow, rank), F32),
        pltpu.VMEM((nx, nz, prow, rank), BF16),
        pltpu.VMEM((nx, nz, prow, rank), BF16),
        pltpu.VMEM((nz, prow, rank), BF16),
        pltpu.VMEM((nz, prow, rank), BF16),
        pltpu.VMEM((ncol, prow, rank), BF16),
        pltpu.VMEM((2, ncol, grow, LANES), F32),
        pltpu.VMEM((ny, 2, grow, LANES), F32),
        pltpu.VMEM((2, ncol, grow, LANES), F32),
        pltpu.VMEM((rank, rank), F32),
        pltpu.VMEM((2, ny, wrow, cols_dev), F32),
        pltpu.VMEM((ny, wrow, cols_dev), BF16),
        pltpu.VMEM((ny, wrow, cols_dev), BF16),
        pltpu.VMEM((ny, wrow, cols_dev), BF16),
        pltpu.VMEM((ny, wrow, cols_dev), BF16),
        pltpu.VMEM((2 * ny, wrow, cols_dev), BF16),
        pltpu.VMEM((rank, cols_dev), F32),
        pltpu.VMEM((1, rank), F32),
        pltpu.VMEM((nx, nz, 1, rank), F32),
        sem(3),
        sem(ny), sem(ny), sem(ny), sem(ny),
        sem(nx, nz), sem(nx, nz), sem(nz), sem(nz), sem(nz), sem(nz), sem(nx, nz), sem(nx, nz),
        sem(ny, 2), sem(ny, 2), sem(nx, nz), sem(nx, nz), sem(1), sem(1),
        sem(2), sem(2), sem(ny, 2), sem(ny, 2), sem(ny, 2), sem(ny, 2), sem(ny), sem(ny),
        sem(nx, nz), sem(nx, nz),
    ]
    momentum, gradient, right_factor = [
        pltpu.with_memory_space_constraint(value, pltpu.HBM) for value in (momentum, gradient, right_factor)
    ]
    whole = pl.BlockSpec(memory_space=pltpu.VMEM)
    hbm = pl.BlockSpec(memory_space=pltpu.HBM)
    buffer, basis, scaled, coeff, new_right = pl.pallas_call(
        functools.partial(step_kernel, (ny, nx, nz, scale)),
        out_shape=[
            jax.ShapeDtypeStruct((rows_dev, cols_dev), BF16),
            jax.ShapeDtypeStruct((rows_dev, rank), BF16),
            jax.ShapeDtypeStruct((rows_dev, rank), BF16),
            jax.ShapeDtypeStruct((rank, cols_dev), BF16),
            jax.ShapeDtypeStruct((frows, rank), F32),
        ],
        in_specs=[hbm] * 3,
        out_specs=[whole] * 5,
        scratch_shapes=scratch,
        compiler_params=pltpu.CompilerParams(
            collective_id=0, has_side_effects=True, vmem_limit_bytes=48 * 1024 * 1024
        ),
        name="panel_and_factor",
    )(momentum, gradient, right_factor)
    step = min(128, rows_dev)
    return pl.pallas_call(
        outputs_kernel,
        out_shape=[jax.ShapeDtypeStruct((rows_dev, cols_dev), BF16)] * 2
        + [jax.ShapeDtypeStruct((frows, rank), F32)],
        in_specs=[whole] * 5,
        out_specs=[hbm] * 3,
        scratch_shapes=[pltpu.VMEM((rows_dev // step, step, cols_dev), BF16)] * 2
        + [sem(2, rows_dev // step), pltpu.SemaphoreType.DMA],
        compiler_params=pltpu.CompilerParams(vmem_limit_bytes=32 * 1024 * 1024),
        name="momentum_and_update",
    )(buffer, basis, scaled, coeff, new_right)


def solution(mesh, nx=X_CHIPS):
    placed = (P("row", "col"), P("row", "col"), P(("col", "row"), None))
    return jax.shard_map(
        functools.partial(body, nx), mesh=mesh, in_specs=placed, out_specs=placed, check_vma=False
    )
```

```python
import functools
import math

import jax
import jax.numpy as jnp
from jax import lax
from jax.experimental import pallas as pl
from jax.experimental.pallas import tpu as pltpu
from jax.sharding import PartitionSpec as P

MESH = pl.DeviceIdType.MESH
LANES = 128
X_CHIPS = 4
F32 = jnp.float32
BF16 = jnp.bfloat16


def dot(a, b):
    return jnp.dot(a, b, preferred_element_type=F32)


def dot_nt(a, b):
    return lax.dot_general(a, b, (((1,), (1,)), ((), ())), preferred_element_type=F32)


def split(value):
    high = value.astype(BF16)
    return high, (value - high.astype(F32)).astype(BF16)


def splat(rows, lane):
    return jnp.broadcast_to(rows[:, lane : lane + 1], (rows.shape[0], LANES))


def eliminate(block, hooks):
    n = LANES
    lanes = lax.broadcasted_iota(jnp.int32, (8, LANES), 1)
    sublane = lax.broadcasted_iota(jnp.int32, (8, LANES), 0)
    groups = [block[8 * g : 8 * g + 8, :] for g in range(n // 8)]
    for j in range(n // 8):
        if j in hooks:
            hooks[j]()
        base = 8 * j
        inside = (lanes >= base) & (lanes < base + 8)
        rows = [jnp.broadcast_to(groups[j][k : k + 1, :], (8, LANES)) for k in range(8)]
        entry = {(i, k): splat(rows[k], base + i) for k in range(8) for i in range(k, 8)}
        rows = [jnp.where(inside, jnp.where(lanes == base + k, 1.0, 0.0), rows[k]) for k in range(8)]
        low, inv = {}, {}
        for k in range(8):
            root = lax.rsqrt(entry[k, k])
            for i in range(k + 1, 8):
                low[i, k] = entry[i, k] * root
            for m in range(k + 1, 8):
                for i in range(m, 8):
                    entry[i, m] = entry[i, m] - low[i, k] * low[m, k]
            rows[k] = rows[k] * root
            for i in range(k + 1, 8):
                rows[i] = rows[i] - low[i, k] * rows[k]
            inv[k, k] = root
            for i in range(k):
                total = low[k, i] * inv[i, i]
                for m in range(i + 1, k):
                    total = total + low[k, m] * inv[m, i]
                inv[k, i] = -(total * root)
        value = rows[0]
        for k in range(1, 8):
            value = jnp.where(sublane == k, rows[k], value)
        groups[j] = value
        if j == n // 8 - 1:
            break
        back = []
        for i in range(8):
            terms = [inv[k, i] * rows[k] for k in range(i, 8)]
            while len(terms) > 1:
                terms = [sum(terms[a : a + 2][1:], terms[a]) for a in range(0, len(terms), 2)]
            back.append(terms[0])
        for g in range(j + 1, n // 8):
            columns = [splat(groups[g], base + k) for k in range(8)]
            terms = [columns[k] * back[k] for k in range(8)]
            while len(terms) > 1:
                terms = [terms[a] + terms[a + 1] for a in range(0, len(terms), 2)]
            groups[g] = jnp.where(inside, 0.0, groups[g]) - terms[0]
    whole = jnp.concatenate(groups, axis=0)
    at_row = lax.broadcasted_iota(jnp.int32, (n, n), 0)
    at_col = lax.broadcasted_iota(jnp.int32, (n, n), 1)
    return jnp.where(at_row >= at_col, whole, 0.0)


def exact(a, b, dims):
    a_high, a_low = split(a)
    b_high, b_low = split(b)
    product = functools.partial(
        lax.dot_general, dimension_numbers=((dims[:1], dims[1:]), ((), ())), preferred_element_type=F32
    )
    return product(a_high, b_high) + (product(a_high, b_low) + product(a_low, b_high))


def inverse_lower(leading, rest, out_ref, early, late):
    top, bottom = slice(0, LANES), slice(LANES, 2 * LANES)
    first = eliminate(leading, {2: early})
    out_ref[top, top] = first
    out_ref[top, bottom] = jnp.zeros((LANES, LANES), F32)
    across, trailing = rest()
    upper = exact(first, across, (1, 1))
    second = eliminate(trailing - exact(upper, upper, (0, 0)), {LANES // 16: late})
    out_ref[bottom, bottom] = second
    out_ref[bottom, top] = -exact(second, exact(upper, first, (0, 0)), (1, 0))


def remote(src, dst, send, recv, device):
    return pltpu.make_async_remote_copy(
        src_ref=src, dst_ref=dst, send_sem=send, recv_sem=recv, device_id=device, device_id_type=MESH
    )


def step_kernel(
    sizes,
    momentum,
    gradient,
    factor,
    buf,
    basis_low,
    scaled_out,
    coeff_low,
    right_out,
    *scratch,
):
    ny, nx, nz, scale = sizes
    (
        grad, fown, fslot, fall, part, psend, xgot, zsend, zgot, panel, panel_t,
        gpart, ggot, gall, lower_inv, wpart, wsib, wsibgot, wsend, wgot, wall, coeff_t,
        nown, ngot,
        local_sem, f_send, f_recv, fs_send, fs_recv,
        x_send, x_recv, z_send, z_recv, pz_send, pz_recv, px_send, px_recv,
        gy_send, gy_recv, gx_send, gx_recv, gs_send, gs_recv,
        ws_send, ws_recv, wy_send, wy_recv, wa_send, wa_recv, wf_send, wf_recv,
        n_send, n_recv,
    ) = scratch
    row, col = lax.axis_index("row"), lax.axis_index("col")
    y, core = row // 2, row % 2
    x, z = col // nz, col % nz
    frows, rank = factor.shape
    rows_dev, cols_dev = buf.shape
    ncol = nx * nz
    sibling = (y * 2 + 1 - core, col)

    def at_y(d, flip=0):
        core_to = core if flip == 0 else 1 - core
        return (lax.rem(y + d, ny) * 2 + core_to, col)

    def at_x(d):
        return (row, lax.rem(x + d, nx) * nz + z)

    def at_z(d):
        return (row, x * nz + lax.rem(z + d, nz))

    def col_of(dx, dz):
        return lax.rem(x + dx + nx, nx) * nz + lax.rem(z + dz + nz, nz)

    def at_xz(dx, dz):
        return (row, col_of(dx, dz))

    started = []

    def send(copy):
        copy.start()
        started.append(copy)

    far_first = sorted(range(1, ny), key=lambda d: -min(d, ny - d))
    near = far_first[::-1]

    loads = [
        pltpu.make_async_copy(momentum, buf, local_sem.at[0]),
        pltpu.make_async_copy(gradient, grad, local_sem.at[1]),
        pltpu.make_async_copy(factor, fown, local_sem.at[2]),
    ]
    for copy in loads[::-1]:
        copy.start()

    peers = [at_y(d, flip) for d in range(ny) for flip in range(2) if (d, flip) != (0, 0)]
    col_peers = [(dx, dz) for dx in range(nx) for dz in range(nz) if (dx, dz) != (0, 0)]
    col_peers.sort(key=lambda d: -min(d[0], nx - d[0]) - min(d[1], nz - d[1]))
    peers += [at_xz(*d) for d in col_peers]
    barrier = pltpu.get_barrier_semaphore()
    for peer in peers:
        pl.semaphore_signal(barrier, inc=1, device_id=peer, device_id_type=MESH)
    loads[2].wait()
    fslot[row] = jnp.concatenate([fown[:, :LANES], fown[:, LANES:]], axis=0).astype(BF16)
    pl.semaphore_wait(barrier, len(peers))

    for d in far_first:
        send(remote(fslot.at[row], fslot.at[row], f_send.at[d], f_recv.at[d], at_y(d)))
    send(remote(fslot.at[row], fslot.at[row], fs_send.at[0], fs_recv.at[0], sibling))
    loads[0].wait()
    loads[1].wait()

    def add_rows(i, carry):
        here = pl.ds(pl.multiple_of(i * 32, 32), 32)
        buf[here, :] = (buf[here, :].astype(F32) + grad[here, :].astype(F32)).astype(BF16)
        return carry

    lax.fori_loop(0, rows_dev // 32, add_rows, 0)

    def unpack(source):
        whole = fslot[source].astype(F32)
        here = pl.ds(pl.multiple_of(source * frows, 8), frows)
        fall[here, :LANES] = whole[:frows]
        fall[here, LANES:] = whole[frows:]

    unpack(row)
    for d in near:
        source = lax.rem(y + ny - d, ny) * 2 + core
        remote(fslot.at[source], fslot.at[source], f_send.at[d], f_recv.at[d], at_y(ny - d)).wait_recv()
        send(remote(fslot.at[source], fslot.at[source], fs_send.at[d], fs_recv.at[d], sibling))
        unpack(source)
    for d in [0] + near:
        source = lax.rem(y + ny - d, ny) * 2 + 1 - core
        remote(fslot.at[source], fslot.at[source], fs_send.at[d], fs_recv.at[d], sibling).wait_recv()
        unpack(source)

    prow = rows_dev // ncol
    right = fall[...].astype(BF16)
    many = rows_dev // nx
    order = sorted(range(1, nz), key=lambda d: -min(d, nz - d)) + [0]
    for dx in list(range(1, nx)) + [0]:
        group = lax.rem(x + dx, nx)
        value = dot(buf[pl.ds(pl.multiple_of(group * many, many), many), :], right).reshape(nz, prow, rank)
        if dx == 0:
            part[...] = value
            continue
        psend[dx] = value.astype(BF16)
        for dz in order:
            src = psend.at[dx, lax.rem(z + dz, nz)]
            send(remote(src, xgot.at[dx, dz], x_send.at[dx, dz], x_recv.at[dx, dz], at_x(dx)))
    for dz in order:
        value = part[lax.rem(z + dz, nz)]
        for dx in range(1, nx):
            remote(xgot.at[dx, dz], xgot.at[dx, dz], x_send.at[dx, dz], x_recv.at[dx, dz], at_x(dx)).wait_recv()
            value = value + xgot[dx, dz].astype(F32)
        if dz:
            zsend[dz] = value.astype(BF16)
            send(remote(zsend.at[dz], zgot.at[dz], z_send.at[dz], z_recv.at[dz], at_z(dz)))
    for dz in sorted(range(1, nz), key=lambda d: min(d, nz - d)):
        remote(zgot.at[dz], zgot.at[dz], z_send.at[dz], z_recv.at[dz], at_z(dz)).wait_recv()
        value = value + zgot[dz].astype(F32)
    panel[col] = value.astype(BF16)
    for dz in order[:-1]:
        send(remote(panel.at[col], panel.at[col], pz_send.at[dz], pz_recv.at[dz], at_z(dz)))
    for dz in [0] + sorted(range(1, nz), key=lambda d: min(d, nz - d)):
        piece = x * nz + lax.rem(z + nz - dz, nz)
        if dz:
            remote(panel.at[piece], panel.at[piece], pz_send.at[dz], pz_recv.at[dz], at_z(dz)).wait_recv()
        for dx in range(1, nx):
            send(remote(panel.at[piece], panel.at[piece], px_send.at[dx, dz], px_recv.at[dx, dz], at_x(dx)))
    for dz in range(nz):
        for dx in range(1, nx):
            piece = lax.rem(x + nx - dx, nx) * nz + lax.rem(z + nz - dz, nz)
            remote(panel.at[piece], panel.at[piece], px_send.at[dx, dz], px_recv.at[dx, dz], at_x(dx)).wait_recv()

    left = panel[...].reshape(rows_dev, rank)
    left_t = left.T
    halves = rank // 2
    panel_t[...] = left_t.reshape(2, halves, rows_dev)

    grow = rank // ncol
    gram = dot(left_t, left)
    for h in range(2):
        gpart[h] = gram[:, h * LANES : (h + 1) * LANES].reshape(ncol, grow, LANES)
    gpeers = [(d, flip) for d in range(ny) for flip in range(2) if (d, flip) != (0, 0)]
    own_half = jnp.where(col < ncol // 2, 0, core)
    for d, flip in gpeers:
        half = own_half if flip == 0 else jnp.where(col < ncol // 2, 0, 1 - core)
        send(remote(gpart.at[half, col], ggot.at[d, flip], gy_send.at[d, flip], gy_recv.at[d, flip], at_y(d, flip)))

    wrow = halves // ny
    tiles = cols_dev // LANES
    cuts = [0, (tiles + 1) // 2 * LANES, cols_dev] if tiles > 1 else [0, cols_dev]
    parts = [pl.ds(a, b - a) for a, b in zip(cuts[:-1], cuts[1:])]
    for p, lot in enumerate(parts):
        value = dot(panel_t[1 - core], buf[:, lot])
        wsib[:, :, lot] = value.astype(BF16).reshape(ny, wrow, lot.size)
        src, dst = wsib.at[:, :, lot], wsibgot.at[:, :, lot]
        send(remote(src, dst, ws_send.at[p], ws_recv.at[p], sibling))

    value = dot(panel_t[core], buf[...])
    wpart[...] = value.reshape(ny, wrow, cols_dev)

    def merged(d, lot):
        piece = lax.rem(y + d, ny)
        return wpart[piece, :, lot] + wsibgot[piece, :, lot].astype(F32)

    def spread(p, lot):
        got = wsibgot.at[:, :, lot]
        remote(got, got, ws_send.at[p], ws_recv.at[p], sibling).wait_recv()
        for d in far_first:
            wsend[d, :, lot] = merged(d, lot).astype(BF16)
            src = wsend.at[d, :, lot]
            send(remote(src, wgot.at[d, :, lot], wy_send.at[d, p], wy_recv.at[d, p], at_y(d)))

    mine = core * ny + y

    def finish(p, lot):
        value = merged(0, lot)
        for d in near:
            got = wgot.at[d, :, lot]
            remote(got, got, wy_send.at[d, p], wy_recv.at[d, p], at_y(d)).wait_recv()
            value = value + wgot[d, :, lot].astype(F32)
        wall[mine, :, lot] = value.astype(BF16)
        block = wall.at[mine, :, lot]
        for d in far_first:
            send(remote(block, block, wa_send.at[d, p], wa_recv.at[d, p], at_y(d)))

    spread(0, parts[0])
    value = gpart[own_half, col]
    for d, flip in gpeers:
        remote(ggot.at[d, flip], ggot.at[d, flip], gy_send.at[d, flip], gy_recv.at[d, flip], at_y(d, flip)).wait_recv()
        value = value + ggot[d, flip]
    gall[core, col] = value
    slice_own = gall.at[core, col]
    for dx, dz in col_peers:
        send(remote(slice_own, slice_own, gx_send.at[dx, dz], gx_recv.at[dx, dz], at_xz(dx, dz)))
    for p, lot in enumerate(parts[1:]):
        spread(p + 1, lot)
    for p, lot in enumerate(parts[:-1]):
        finish(p, lot)
    for dx, dz in col_peers[::-1]:
        piece = gall.at[core, col_of(-dx, -dz)]
        remote(piece, piece, gx_send.at[dx, dz], gx_recv.at[dx, dz], at_xz(dx, dz)).wait_recv()
    lower_rows = pl.ds(ncol // 2, ncol // 2)
    ours, theirs = gall.at[core, lower_rows], gall.at[1 - core, lower_rows]
    send(remote(ours, ours, gs_send.at[0], gs_recv.at[0], sibling))

    def rest():
        remote(theirs, theirs, gs_send.at[0], gs_recv.at[0], sibling).wait_recv()
        return [gall[h, lower_rows].reshape(LANES, LANES) for h in range(2)]

    def finish_last():
        finish(len(parts) - 1, parts[-1])
        send(remote(wall.at[mine], wall.at[mine], wf_send.at[0], wf_recv.at[0], sibling))

    def arrive(d):
        piece = core * ny + lax.rem(y + ny - d, ny)
        for p, lot in enumerate(parts):
            block = wall.at[piece, :, lot]
            remote(block, block, wa_send.at[d, p], wa_recv.at[d, p], at_y(d)).wait_recv()
        send(remote(wall.at[piece], wall.at[piece], wf_send.at[d], wf_recv.at[d], sibling))

    def forward():
        for d in near:
            arrive(d)

    leading = gall[core, pl.ds(0, ncol // 2)].reshape(LANES, LANES)
    inverse_lower(leading, rest, lower_inv, finish_last, forward)
    high, low = split(lower_inv[...])
    for d in range(ny):
        piece = (1 - core) * ny + lax.rem(y + ny - d, ny)
        remote(wall.at[piece], wall.at[piece], wf_send.at[d], wf_recv.at[d], sibling).wait_recv()

    together = wall[...].reshape(rank, cols_dev)
    coeff_t[...] = dot(high, together) + dot(low, together)
    squares = jnp.zeros((rank, LANES), F32)
    for i in range(cols_dev // LANES):
        value = coeff_t[:, i * LANES : (i + 1) * LANES]
        squares = squares + value * value
    value = jnp.sum(squares.T, axis=0, keepdims=True)
    nown[...] = value
    for dx, dz in col_peers:
        send(remote(nown, ngot.at[dx, dz], n_send.at[dx, dz], n_recv.at[dx, dz], at_xz(dx, dz)))
    coeff_low[...] = coeff_t[...].astype(BF16)
    basis = dot_nt(left, high) + dot_nt(left, low)
    basis_low[...] = basis.astype(BF16)
    begin = row * frows
    if cols_dev >= 2 * LANES:
        tile = jnp.minimum(begin // LANES, cols_dev // LANES - 2)
        near = coeff_t[:, pl.ds(pl.multiple_of(tile * LANES, LANES), 2 * LANES)]
        near = pltpu.roll(near, 2 * LANES - (begin - tile * LANES), axis=1)
    else:
        near = pltpu.roll(coeff_t[...], cols_dev - begin, axis=1)
    mine = near[:, :LANES].T[:frows]
    for copy in started:
        copy.wait_send()
    for dx, dz in col_peers[::-1]:
        got = ngot.at[dx, dz]
        remote(got, got, n_send.at[dx, dz], n_recv.at[dx, dz], at_xz(dx, dz)).wait_recv()
        value = value + ngot[dx, dz]
    inverse = 1.0 / jnp.sqrt(value + 1e-06)
    right_out[...] = mine * inverse
    scaled_out[...] = (basis * (inverse * scale)).astype(BF16)


def outputs_kernel(
    buffer, basis, scaled, coeff, right, momentum_out, update_out, right_out, momentum_low, update_low, sems, right_sem
):
    rows = momentum_low.shape[1]
    copies = [pltpu.make_async_copy(right, right_out, right_sem)]
    copies[0].start()
    for i in range(buffer.shape[0] // rows):
        here = slice(i * rows, (i + 1) * rows)
        update_low[i] = dot(scaled[here, :], coeff[...]).astype(BF16)
        copies.append(pltpu.make_async_copy(update_low.at[i], update_out.at[here], sems.at[0, i]))
        copies[-1].start()
        correction = dot(basis[here, :], coeff[...])
        momentum_low[i] = (buffer[here, :].astype(F32) - 0.05 * correction).astype(BF16)
        copies.append(pltpu.make_async_copy(momentum_low.at[i], momentum_out.at[here], sems.at[1, i]))
        copies[-1].start()
    for copy in copies:
        copy.wait()


def body(nx, momentum, gradient, right_factor):
    ny = lax.axis_size("row") // 2
    nz = lax.axis_size("col") // nx
    ncol = nx * nz
    rows_dev, cols_dev = momentum.shape
    frows, rank = right_factor.shape
    scale = math.sqrt(rows_dev * 2 * ny * cols_dev * ncol / rank)
    prow, grow, wrow = rows_dev // ncol, rank // ncol, rank // (2 * ny)
    sem = lambda *shape: pltpu.SemaphoreType.DMA(shape)
    scratch = [
        pltpu.VMEM((rows_dev, cols_dev), BF16),
        pltpu.VMEM((frows, rank), F32),
        pltpu.VMEM((2 * ny, 2 * frows, LANES), BF16),
        pltpu.VMEM((cols_dev, rank), F32),
        pltpu.VMEM((nz, prow, rank), F32),
        pltpu.VMEM((nx, nz, prow, rank), BF16),
        pltpu.VMEM((nx, nz, prow, rank), BF16),
        pltpu.VMEM((nz, prow, rank), BF16),
        pltpu.VMEM((nz, prow, rank), BF16),
        pltpu.VMEM((ncol, prow, rank), BF16),
        pltpu.VMEM((2, rank // 2, rows_dev), BF16),
        pltpu.VMEM((2, ncol, grow, LANES), F32),
        pltpu.VMEM((ny, 2, grow, LANES), F32),
        pltpu.VMEM((2, ncol, grow, LANES), F32),
        pltpu.VMEM((rank, rank), F32),
        pltpu.VMEM((ny, wrow, cols_dev), F32),
        pltpu.VMEM((ny, wrow, cols_dev), BF16),
        pltpu.VMEM((ny, wrow, cols_dev), BF16),
        pltpu.VMEM((ny, wrow, cols_dev), BF16),
        pltpu.VMEM((ny, wrow, cols_dev), BF16),
        pltpu.VMEM((2 * ny, wrow, cols_dev), BF16),
        pltpu.VMEM((rank, cols_dev), F32),
        pltpu.VMEM((1, rank), F32),
        pltpu.VMEM((nx, nz, 1, rank), F32),
        sem(3),
        sem(ny), sem(ny), sem(ny), sem(ny),
        sem(nx, nz), sem(nx, nz), sem(nz), sem(nz), sem(nz), sem(nz), sem(nx, nz), sem(nx, nz),
        sem(ny, 2), sem(ny, 2), sem(nx, nz), sem(nx, nz), sem(1), sem(1),
        sem(2), sem(2), sem(ny, 2), sem(ny, 2), sem(ny, 2), sem(ny, 2), sem(ny), sem(ny),
        sem(nx, nz), sem(nx, nz),
    ]
    momentum, gradient, right_factor = [
        pltpu.with_memory_space_constraint(value, pltpu.HBM) for value in (momentum, gradient, right_factor)
    ]
    whole = pl.BlockSpec(memory_space=pltpu.VMEM)
    hbm = pl.BlockSpec(memory_space=pltpu.HBM)
    buffer, basis, scaled, coeff, new_right = pl.pallas_call(
        functools.partial(step_kernel, (ny, nx, nz, scale)),
        out_shape=[
            jax.ShapeDtypeStruct((rows_dev, cols_dev), BF16),
            jax.ShapeDtypeStruct((rows_dev, rank), BF16),
            jax.ShapeDtypeStruct((rows_dev, rank), BF16),
            jax.ShapeDtypeStruct((rank, cols_dev), BF16),
            jax.ShapeDtypeStruct((frows, rank), F32),
        ],
        in_specs=[hbm] * 3,
        out_specs=[whole] * 5,
        scratch_shapes=scratch,
        compiler_params=pltpu.CompilerParams(
            collective_id=0, has_side_effects=True, vmem_limit_bytes=48 * 1024 * 1024
        ),
        name="panel_and_factor",
    )(momentum, gradient, right_factor)
    step = min(128, rows_dev)
    return pl.pallas_call(
        outputs_kernel,
        out_shape=[jax.ShapeDtypeStruct((rows_dev, cols_dev), BF16)] * 2
        + [jax.ShapeDtypeStruct((frows, rank), F32)],
        in_specs=[whole] * 5,
        out_specs=[hbm] * 3,
        scratch_shapes=[pltpu.VMEM((rows_dev // step, step, cols_dev), BF16)] * 2
        + [sem(2, rows_dev // step), pltpu.SemaphoreType.DMA],
        compiler_params=pltpu.CompilerParams(vmem_limit_bytes=32 * 1024 * 1024),
        name="momentum_and_update",
    )(buffer, basis, scaled, coeff, new_right)


def solution(mesh, nx=X_CHIPS):
    placed = (P("row", "col"), P("row", "col"), P(("col", "row"), None))
    return jax.shard_map(
        functools.partial(body, nx), mesh=mesh, in_specs=placed, out_specs=placed, check_vma=False
    )
```

```python
import functools
import math

import jax
import jax.numpy as jnp
from jax import lax
from jax.experimental import pallas as pl
from jax.experimental.pallas import tpu as pltpu
from jax.sharding import PartitionSpec as P

MESH = pl.DeviceIdType.MESH
LANES = 128
X_CHIPS = 4
F32 = jnp.float32
BF16 = jnp.bfloat16


def dot(a, b):
    return jnp.dot(a, b, preferred_element_type=F32)


def dot_nt(a, b):
    return lax.dot_general(a, b, (((1,), (1,)), ((), ())), preferred_element_type=F32)


def split(value):
    high = value.astype(BF16)
    return high, (value - high.astype(F32)).astype(BF16)


def splat(rows, lane):
    return jnp.broadcast_to(rows[:, lane : lane + 1], (rows.shape[0], LANES))


def eliminate(block, hook=None):
    n = LANES
    lanes = lax.broadcasted_iota(jnp.int32, (8, LANES), 1)
    sublane = lax.broadcasted_iota(jnp.int32, (8, LANES), 0)
    groups = [block[8 * g : 8 * g + 8, :] for g in range(n // 8)]
    for j in range(n // 8):
        if hook is not None and j == n // 16:
            hook()
        base = 8 * j
        inside = (lanes >= base) & (lanes < base + 8)
        rows = [jnp.broadcast_to(groups[j][k : k + 1, :], (8, LANES)) for k in range(8)]
        entry = {(i, k): splat(rows[k], base + i) for k in range(8) for i in range(k, 8)}
        rows = [jnp.where(inside, jnp.where(lanes == base + k, 1.0, 0.0), rows[k]) for k in range(8)]
        low, inv = {}, {}
        for k in range(8):
            root = lax.rsqrt(entry[k, k])
            for i in range(k + 1, 8):
                low[i, k] = entry[i, k] * root
            for m in range(k + 1, 8):
                for i in range(m, 8):
                    entry[i, m] = entry[i, m] - low[i, k] * low[m, k]
            rows[k] = rows[k] * root
            for i in range(k + 1, 8):
                rows[i] = rows[i] - low[i, k] * rows[k]
            inv[k, k] = root
            for i in range(k):
                total = low[k, i] * inv[i, i]
                for m in range(i + 1, k):
                    total = total + low[k, m] * inv[m, i]
                inv[k, i] = -(total * root)
        value = rows[0]
        for k in range(1, 8):
            value = jnp.where(sublane == k, rows[k], value)
        groups[j] = value
        if j == n // 8 - 1:
            break
        back = []
        for i in range(8):
            terms = [inv[k, i] * rows[k] for k in range(i, 8)]
            while len(terms) > 1:
                terms = [sum(terms[a : a + 2][1:], terms[a]) for a in range(0, len(terms), 2)]
            back.append(terms[0])
        for g in range(j + 1, n // 8):
            columns = [splat(groups[g], base + k) for k in range(8)]
            terms = [columns[k] * back[k] for k in range(8)]
            while len(terms) > 1:
                terms = [terms[a] + terms[a + 1] for a in range(0, len(terms), 2)]
            groups[g] = jnp.where(inside, 0.0, groups[g]) - terms[0]
    whole = jnp.concatenate(groups, axis=0)
    at_row = lax.broadcasted_iota(jnp.int32, (n, n), 0)
    at_col = lax.broadcasted_iota(jnp.int32, (n, n), 1)
    return jnp.where(at_row >= at_col, whole, 0.0)


def exact(a, b, dims):
    a_high, a_low = split(a)
    b_high, b_low = split(b)
    product = functools.partial(
        lax.dot_general, dimension_numbers=((dims[:1], dims[1:]), ((), ())), preferred_element_type=F32
    )
    return product(a_high, b_high) + (product(a_high, b_low) + product(a_low, b_high))


def inverse_lower(work, out_ref, hook):
    top, rest = slice(0, LANES), slice(LANES, 2 * LANES)
    first = eliminate(work[top, top])
    out_ref[top, top] = first
    out_ref[top, rest] = jnp.zeros((LANES, LANES), F32)
    upper = exact(first, work[top, rest], (1, 0))
    schur = work[rest, rest] - exact(upper, upper, (0, 0))
    second = eliminate(schur, hook)
    out_ref[rest, rest] = second
    out_ref[rest, top] = -exact(second, exact(upper, first, (0, 0)), (1, 0))


def remote(src, dst, send, recv, device):
    return pltpu.make_async_remote_copy(
        src_ref=src, dst_ref=dst, send_sem=send, recv_sem=recv, device_id=device, device_id_type=MESH
    )


def step_kernel(
    sizes,
    momentum,
    gradient,
    factor,
    buf,
    basis_low,
    scaled_out,
    coeff_low,
    right_out,
    *scratch,
):
    ny, nx, nz, scale = sizes
    (
        grad, fown, fslot, fall, part, psend, xgot, panel, panel_t,
        gpart, ggot, gall, work, lower_inv, wpart, wsib, wsibgot, wsend, wgot, wall, coeff_t,
        nown, ngot,
        local_sem, f_send, f_recv, fs_send, fs_recv,
        x_send, x_recv, px_send, px_recv,
        gy_send, gy_recv, gx_send, gx_recv, gs_send, gs_recv,
        ws_send, ws_recv, wy_send, wy_recv, wa_send, wa_recv, wf_send, wf_recv,
        n_send, n_recv,
    ) = scratch
    row, col = lax.axis_index("row"), lax.axis_index("col")
    y, core = row // 2, row % 2
    x, z = col // nz, col % nz
    frows, rank = factor.shape
    rows_dev, cols_dev = buf.shape
    ncol = nx * nz
    sibling = (y * 2 + 1 - core, col)

    def at_y(d, flip=0):
        core_to = core if flip == 0 else 1 - core
        return (lax.rem(y + d, ny) * 2 + core_to, col)

    def at_x(d):
        return (row, lax.rem(x + d, nx) * nz + z)

    def at_z(d):
        return (row, x * nz + lax.rem(z + d, nz))

    def col_of(dx, dz):
        return lax.rem(x + dx + nx, nx) * nz + lax.rem(z + dz + nz, nz)

    def at_xz(dx, dz):
        return (row, col_of(dx, dz))

    started = []

    def send(copy):
        copy.start()
        started.append(copy)

    far_first = sorted(range(1, ny), key=lambda d: -min(d, ny - d))
    near = far_first[::-1]

    loads = [
        pltpu.make_async_copy(momentum, buf, local_sem.at[0]),
        pltpu.make_async_copy(gradient, grad, local_sem.at[1]),
        pltpu.make_async_copy(factor, fown, local_sem.at[2]),
    ]
    for copy in loads[::-1]:
        copy.start()

    peers = [at_y(d, flip) for d in range(ny) for flip in range(2) if (d, flip) != (0, 0)]
    col_peers = [(dx, dz) for dx in range(nx) for dz in range(nz) if (dx, dz) != (0, 0)]
    col_peers.sort(key=lambda d: -min(d[0], nx - d[0]) - min(d[1], nz - d[1]))
    peers += [at_xz(*d) for d in col_peers]
    barrier = pltpu.get_barrier_semaphore()
    for peer in peers:
        pl.semaphore_signal(barrier, inc=1, device_id=peer, device_id_type=MESH)
    loads[2].wait()
    fslot[row] = jnp.concatenate([fown[:, :LANES], fown[:, LANES:]], axis=0).astype(BF16)
    pl.semaphore_wait(barrier, len(peers))

    for d in far_first:
        send(remote(fslot.at[row], fslot.at[row], f_send.at[d], f_recv.at[d], at_y(d)))
    send(remote(fslot.at[row], fslot.at[row], fs_send.at[0], fs_recv.at[0], sibling))
    loads[0].wait()
    loads[1].wait()

    def add_rows(i, carry):
        here = pl.ds(pl.multiple_of(i * 32, 32), 32)
        buf[here, :] = (buf[here, :].astype(F32) + grad[here, :].astype(F32)).astype(BF16)
        return carry

    lax.fori_loop(0, rows_dev // 32, add_rows, 0)

    def unpack(source):
        whole = fslot[source].astype(F32)
        here = pl.ds(pl.multiple_of(source * frows, 8), frows)
        fall[here, :LANES] = whole[:frows]
        fall[here, LANES:] = whole[frows:]

    unpack(row)
    for d in near:
        source = lax.rem(y + ny - d, ny) * 2 + core
        remote(fslot.at[source], fslot.at[source], f_send.at[d], f_recv.at[d], at_y(ny - d)).wait_recv()
        send(remote(fslot.at[source], fslot.at[source], fs_send.at[d], fs_recv.at[d], sibling))
        unpack(source)
    for d in [0] + near:
        source = lax.rem(y + ny - d, ny) * 2 + 1 - core
        remote(fslot.at[source], fslot.at[source], fs_send.at[d], fs_recv.at[d], sibling).wait_recv()
        unpack(source)

    prow = rows_dev // ncol
    right = fall[...].astype(BF16)
    many = rows_dev // nx
    for dx in sorted(range(nx), key=lambda d: -min(d, nx - d)):
        group = lax.rem(x + dx, nx)
        value = dot(buf[pl.ds(pl.multiple_of(group * many, many), many), :], right).reshape(nz, prow, rank)
        if dx == 0:
            part[...] = value
        psend[dx] = value.astype(BF16)
        for dz in sorted(range(nz), key=lambda d: -min(d, nz - d)):
            if (dx, dz) != (0, 0):
                src, dst = psend.at[dx, lax.rem(z + dz, nz)], xgot.at[dx, dz]
                send(remote(src, dst, x_send.at[dx, dz], x_recv.at[dx, dz], at_xz(dx, dz)))
    value = part[z]
    for dx, dz in col_peers[::-1]:
        got = xgot.at[dx, dz]
        remote(got, got, x_send.at[dx, dz], x_recv.at[dx, dz], at_xz(dx, dz)).wait_recv()
        value = value + xgot[dx, dz].astype(F32)
    panel[col] = value.astype(BF16)
    for dx, dz in col_peers:
        block = panel.at[col]
        send(remote(block, block, px_send.at[dx, dz], px_recv.at[dx, dz], at_xz(dx, dz)))
    for dx, dz in col_peers[::-1]:
        block = panel.at[col_of(-dx, -dz)]
        remote(block, block, px_send.at[dx, dz], px_recv.at[dx, dz], at_xz(dx, dz)).wait_recv()

    left = panel[...].reshape(rows_dev, rank)
    left_t = left.T
    halves = rank // 2
    panel_t[...] = left_t.reshape(2, halves, rows_dev)

    grow = rank // ncol
    gram = dot(left_t, left)
    for h in range(2):
        gpart[h] = gram[:, h * LANES : (h + 1) * LANES].reshape(ncol, grow, LANES)
    gpeers = [(d, flip) for d in range(ny) for flip in range(2) if (d, flip) != (0, 0)]
    for d, flip in gpeers:
        half = core if flip == 0 else 1 - core
        send(remote(gpart.at[half, col], ggot.at[d, flip], gy_send.at[d, flip], gy_recv.at[d, flip], at_y(d, flip)))

    wrow = halves // ny
    tiles = cols_dev // LANES
    cuts = [0, (tiles + 1) // 2 * LANES, cols_dev] if tiles > 1 else [0, cols_dev]
    parts = [pl.ds(a, b - a) for a, b in zip(cuts[:-1], cuts[1:])]
    for p, lot in enumerate(parts):
        value = dot(panel_t[1 - core], buf[:, lot])
        wsib[:, :, lot] = value.astype(BF16).reshape(ny, wrow, lot.size)
        src, dst = wsib.at[:, :, lot], wsibgot.at[:, :, lot]
        send(remote(src, dst, ws_send.at[p], ws_recv.at[p], sibling))

    value = dot(panel_t[core], buf[...])
    wpart[...] = value.reshape(ny, wrow, cols_dev)

    def merged(d, lot):
        piece = lax.rem(y + d, ny)
        return wpart[piece, :, lot] + wsibgot[piece, :, lot].astype(F32)

    def spread(p, lot):
        got = wsibgot.at[:, :, lot]
        remote(got, got, ws_send.at[p], ws_recv.at[p], sibling).wait_recv()
        for d in far_first:
            wsend[d, :, lot] = merged(d, lot).astype(BF16)
            src = wsend.at[d, :, lot]
            send(remote(src, wgot.at[d, :, lot], wy_send.at[d, p], wy_recv.at[d, p], at_y(d)))

    mine = core * ny + y

    def finish(p, lot):
        value = merged(0, lot)
        for d in near:
            got = wgot.at[d, :, lot]
            remote(got, got, wy_send.at[d, p], wy_recv.at[d, p], at_y(d)).wait_recv()
            value = value + wgot[d, :, lot].astype(F32)
        wall[mine, :, lot] = value.astype(BF16)
        block = wall.at[mine, :, lot]
        for d in far_first:
            send(remote(block, block, wa_send.at[d, p], wa_recv.at[d, p], at_y(d)))

    spread(0, parts[0])
    value = gpart[core, col]
    for d, flip in gpeers:
        remote(ggot.at[d, flip], ggot.at[d, flip], gy_send.at[d, flip], gy_recv.at[d, flip], at_y(d, flip)).wait_recv()
        value = value + ggot[d, flip]
    gall[core, col] = value
    slice_own = gall.at[core, col]
    for dx, dz in col_peers:
        send(remote(slice_own, slice_own, gx_send.at[dx, dz], gx_recv.at[dx, dz], at_xz(dx, dz)))
    for p, lot in enumerate(parts[1:]):
        spread(p + 1, lot)
    for p, lot in enumerate(parts[:-1]):
        finish(p, lot)
    for dx, dz in col_peers[::-1]:
        piece = gall.at[core, col_of(-dx, -dz)]
        remote(piece, piece, gx_send.at[dx, dz], gx_recv.at[dx, dz], at_xz(dx, dz)).wait_recv()
    send(remote(gall.at[core], gall.at[core], gs_send.at[0], gs_recv.at[0], sibling))
    finish(len(parts) - 1, parts[-1])
    send(remote(wall.at[mine], wall.at[mine], wf_send.at[0], wf_recv.at[0], sibling))
    remote(gall.at[1 - core], gall.at[1 - core], gs_send.at[0], gs_recv.at[0], sibling).wait_recv()
    for h in range(2):
        work[:, h * LANES : (h + 1) * LANES] = gall[h].reshape(rank, LANES)

    def arrive(d):
        piece = core * ny + lax.rem(y + ny - d, ny)
        for p, lot in enumerate(parts):
            block = wall.at[piece, :, lot]
            remote(block, block, wa_send.at[d, p], wa_recv.at[d, p], at_y(d)).wait_recv()
        send(remote(wall.at[piece], wall.at[piece], wf_send.at[d], wf_recv.at[d], sibling))

    def forward():
        for d in near:
            arrive(d)

    inverse_lower(work, lower_inv, forward)
    high, low = split(lower_inv[...])
    for d in range(ny):
        piece = (1 - core) * ny + lax.rem(y + ny - d, ny)
        remote(wall.at[piece], wall.at[piece], wf_send.at[d], wf_recv.at[d], sibling).wait_recv()

    together = wall[...].reshape(rank, cols_dev)
    coeff_t[...] = dot(high, together) + dot(low, together)
    squares = jnp.zeros((rank, LANES), F32)
    for i in range(cols_dev // LANES):
        value = coeff_t[:, i * LANES : (i + 1) * LANES]
        squares = squares + value * value
    value = jnp.sum(squares.T, axis=0, keepdims=True)
    nown[...] = value
    for dx, dz in col_peers:
        send(remote(nown, ngot.at[dx, dz], n_send.at[dx, dz], n_recv.at[dx, dz], at_xz(dx, dz)))
    coeff_low[...] = coeff_t[...].astype(BF16)
    basis = dot_nt(left, high) + dot_nt(left, low)
    basis_low[...] = basis.astype(BF16)
    begin = row * frows
    if cols_dev >= 2 * LANES:
        tile = jnp.minimum(begin // LANES, cols_dev // LANES - 2)
        near = coeff_t[:, pl.ds(pl.multiple_of(tile * LANES, LANES), 2 * LANES)]
        near = pltpu.roll(near, 2 * LANES - (begin - tile * LANES), axis=1)
    else:
        near = pltpu.roll(coeff_t[...], cols_dev - begin, axis=1)
    mine = near[:, :LANES].T[:frows]
    for copy in started:
        copy.wait_send()
    for dx, dz in col_peers[::-1]:
        got = ngot.at[dx, dz]
        remote(got, got, n_send.at[dx, dz], n_recv.at[dx, dz], at_xz(dx, dz)).wait_recv()
        value = value + ngot[dx, dz]
    inverse = 1.0 / jnp.sqrt(value + 1e-06)
    right_out[...] = mine * inverse
    scaled_out[...] = (basis * (inverse * scale)).astype(BF16)


def outputs_kernel(
    buffer, basis, scaled, coeff, right, momentum_out, update_out, right_out, momentum_low, update_low, sems, right_sem
):
    rows = momentum_low.shape[1]
    copies = [pltpu.make_async_copy(right, right_out, right_sem)]
    copies[0].start()
    for i in range(buffer.shape[0] // rows):
        here = slice(i * rows, (i + 1) * rows)
        update_low[i] = dot(scaled[here, :], coeff[...]).astype(BF16)
        copies.append(pltpu.make_async_copy(update_low.at[i], update_out.at[here], sems.at[0, i]))
        copies[-1].start()
        correction = dot(basis[here, :], coeff[...])
        momentum_low[i] = (buffer[here, :].astype(F32) - 0.05 * correction).astype(BF16)
        copies.append(pltpu.make_async_copy(momentum_low.at[i], momentum_out.at[here], sems.at[1, i]))
        copies[-1].start()
    for copy in copies:
        copy.wait()


def body(nx, momentum, gradient, right_factor):
    ny = lax.axis_size("row") // 2
    nz = lax.axis_size("col") // nx
    ncol = nx * nz
    rows_dev, cols_dev = momentum.shape
    frows, rank = right_factor.shape
    scale = math.sqrt(rows_dev * 2 * ny * cols_dev * ncol / rank)
    prow, grow, wrow = rows_dev // ncol, rank // ncol, rank // (2 * ny)
    sem = lambda *shape: pltpu.SemaphoreType.DMA(shape)
    scratch = [
        pltpu.VMEM((rows_dev, cols_dev), BF16),
        pltpu.VMEM((frows, rank), F32),
        pltpu.VMEM((2 * ny, 2 * frows, LANES), BF16),
        pltpu.VMEM((cols_dev, rank), F32),
        pltpu.VMEM((nz, prow, rank), F32),
        pltpu.VMEM((nx, nz, prow, rank), BF16),
        pltpu.VMEM((nx, nz, prow, rank), BF16),
        pltpu.VMEM((ncol, prow, rank), BF16),
        pltpu.VMEM((2, rank // 2, rows_dev), BF16),
        pltpu.VMEM((2, ncol, grow, LANES), F32),
        pltpu.VMEM((ny, 2, grow, LANES), F32),
        pltpu.VMEM((2, ncol, grow, LANES), F32),
        pltpu.VMEM((rank, rank), F32),
        pltpu.VMEM((rank, rank), F32),
        pltpu.VMEM((ny, wrow, cols_dev), F32),
        pltpu.VMEM((ny, wrow, cols_dev), BF16),
        pltpu.VMEM((ny, wrow, cols_dev), BF16),
        pltpu.VMEM((ny, wrow, cols_dev), BF16),
        pltpu.VMEM((ny, wrow, cols_dev), BF16),
        pltpu.VMEM((2 * ny, wrow, cols_dev), BF16),
        pltpu.VMEM((rank, cols_dev), F32),
        pltpu.VMEM((1, rank), F32),
        pltpu.VMEM((nx, nz, 1, rank), F32),
        sem(3),
        sem(ny), sem(ny), sem(ny), sem(ny),
        sem(nx, nz), sem(nx, nz), sem(nx, nz), sem(nx, nz),
        sem(ny, 2), sem(ny, 2), sem(nx, nz), sem(nx, nz), sem(1), sem(1),
        sem(2), sem(2), sem(ny, 2), sem(ny, 2), sem(ny, 2), sem(ny, 2), sem(ny), sem(ny),
        sem(nx, nz), sem(nx, nz),
    ]
    momentum, gradient, right_factor = [
        pltpu.with_memory_space_constraint(value, pltpu.HBM) for value in (momentum, gradient, right_factor)
    ]
    whole = pl.BlockSpec(memory_space=pltpu.VMEM)
    hbm = pl.BlockSpec(memory_space=pltpu.HBM)
    buffer, basis, scaled, coeff, new_right = pl.pallas_call(
        functools.partial(step_kernel, (ny, nx, nz, scale)),
        out_shape=[
            jax.ShapeDtypeStruct((rows_dev, cols_dev), BF16),
            jax.ShapeDtypeStruct((rows_dev, rank), BF16),
            jax.ShapeDtypeStruct((rows_dev, rank), BF16),
            jax.ShapeDtypeStruct((rank, cols_dev), BF16),
            jax.ShapeDtypeStruct((frows, rank), F32),
        ],
        in_specs=[hbm] * 3,
        out_specs=[whole] * 5,
        scratch_shapes=scratch,
        compiler_params=pltpu.CompilerParams(
            collective_id=0, has_side_effects=True, vmem_limit_bytes=48 * 1024 * 1024
        ),
        name="panel_and_factor",
    )(momentum, gradient, right_factor)
    step = min(128, rows_dev)
    return pl.pallas_call(
        outputs_kernel,
        out_shape=[jax.ShapeDtypeStruct((rows_dev, cols_dev), BF16)] * 2
        + [jax.ShapeDtypeStruct((frows, rank), F32)],
        in_specs=[whole] * 5,
        out_specs=[hbm] * 3,
        scratch_shapes=[pltpu.VMEM((rows_dev // step, step, cols_dev), BF16)] * 2
        + [sem(2, rows_dev // step), pltpu.SemaphoreType.DMA],
        compiler_params=pltpu.CompilerParams(vmem_limit_bytes=32 * 1024 * 1024),
        name="momentum_and_update",
    )(buffer, basis, scaled, coeff, new_right)


def solution(mesh, nx=X_CHIPS):
    placed = (P("row", "col"), P("row", "col"), P(("col", "row"), None))
    return jax.shard_map(
        functools.partial(body, nx), mesh=mesh, in_specs=placed, out_specs=placed, check_vma=False
    )
```
